128 devices in a mesh: lon: 16 (over y, x_hi, core), lat: 8 (over x_lo, z).
Axes of the slice: x: 4 (x_hi: 2, x_lo: 2; x = x_hi * 2 + x_lo), y: 4, z: 4, core: 2. Of those that a mesh axis runs over, the one named last changes fastest.
Arguments:
- tracers: float32 [6, 24, 512, 2048], P(None, None, 'lat', 'lon'), may hold values from -6 to 6
- flow_east: float32 [24, 512, 2048], P(None, 'lat', 'lon'), may hold values from -0.35 to 0.35
- flow_north: float32 [24, 512, 2048], P(None, 'lat', 'lon'), may hold values from -0.35 to 0.35
- sea_mask: int32 [24, 512, 2048], P(None, 'lat', 'lon'), may hold values 0 or 1
- atm_fields: bfloat16 [4, 1048576], P(None, ('lon', 'lat')), may hold values from -6 to 6
- remap_weights: bfloat16 [32768, 128, 128], P(('lon', 'lat')), may hold values from -0.5 to 0.5
- remap_src: int32 [32768], P(('lon', 'lat')), may hold values from 0 to 63
- remap_dst: int32 [32768], P(('lon', 'lat')), may hold values from 0 to 8191, as said below
- fold_partner: int32 [2048], P('lon'), may hold values from 0 to 2047, as said below
Outputs:
- forcing: float32 [4, 512, 2048], P(None, 'lat', 'lon')
- tracers_next: float32 [6, 24, 512, 2048], P(None, None, 'lat', 'lon')
The draws below stay inside these ranges and needn't reach their ends.
Inputs may be any that keep to these rules, and one draw needn't show every extreme that they name: `remap_dst`: the weight blocks held by one device name at most 4 destination blocks on any one device; in every draw one device is named 4 times by the blocks of every device. fold_partner[i] = (c - i) mod 2048 for one c.
All inputs are finite; a program needn't handle non-finite values. No bound on the sum of `sea_mask` on one device may be relied on, other than what follows from the above.
Results may differ from the reference program's by a relative error of at most 0.0003.
Values sent between devices are 32-bit elements; how exact they have to be, the bound alone decides.
No kernel may reach another device: no remote copies, remote signals or barrier semaphores. Data moves between devices by JAX's collectives and lax.ppermute only.
A program may use at most 192 MiB of HBM per device.

```python
import jax
import jax.numpy as jnp
from jax import lax

CI = 128
CJ = 64
K = 24
NTR = 6
NF = 4
WB_DEV = 256
ABLK_DEV = 64
CAP = 4
NJ = 512
NI = 2048
NW = 32768
NA = 1048576
N_LON = 16
N_LAT = 8


def draw_remap_dst(key, part):
    key = jax.random.fold_in(key, 11)
    devices = N_LON * N_LAT
    slots = devices * CAP
    busiest = jax.random.randint(jax.random.fold_in(key, 1), (), 0, devices)

    def one_source(source):
        source_key = jax.random.fold_in(key, 100 + source)
        first_key, second_key, third_key = jax.random.split(source_key, 3)
        scores = jax.random.permutation(first_key, slots)
        slot_owner = jnp.arange(slots) // CAP
        scores = scores + jnp.where(slot_owner == busiest, 4 * slots, 0)
        _, chosen = lax.top_k(scores, WB_DEV)
        chosen = jax.random.permutation(second_key, chosen)
        owner = chosen // CAP
        local_row = jax.random.randint(third_key, (WB_DEV,), 0, CJ)
        owner_lon = owner // N_LAT
        owner_lat = owner % N_LAT
        return ((owner_lat * CJ + local_row) * N_LON + owner_lon).astype(jnp.int32)
    return jax.vmap(one_source)(jnp.arange(devices)).reshape(-1)


def draw_fold_partner(key, part):
    key = jax.random.fold_in(key, 23)
    pivot = jax.random.randint(key, (), 0, NI)
    return ((pivot - jnp.arange(NI)) % NI).astype(jnp.int32)


def set_ends(entries, rng, smallest, top_value):
    index_at = [jax.random.randint(jax.random.fold_in(rng, axis), (), 0, length) for axis, length in enumerate(entries.shape)]
    longest = entries.shape.index(max(entries.shape))
    beside = index_at[:longest] + [(index_at[longest] + 1) % entries.shape[longest]] + index_at[longest + 1:]
    return entries.at[tuple(index_at)].set(smallest).at[tuple(beside)].set(top_value)


def steps_of(key, dims, shards, low, largest):
    factor_of = 1.0
    for axis_at, parts in shards:
        draws = jax.random.uniform(jax.random.fold_in(jax.random.fold_in(key, 6), axis_at), (parts,), jnp.float32, low / len(shards), largest / len(shards))
        factor_of = factor_of * jnp.repeat(jnp.exp(draws), dims[axis_at] // parts).reshape((-1,) + (1,) * (len(dims) - 1 - axis_at))
    return factor_of


def noise(own_key, extent, scale, most, pieces=(), held_as=jnp.bfloat16):
    factor_of = steps_of(own_key, extent, pieces, -0.22, 0.18) if pieces else 1.0
    values = jax.random.normal(own_key, extent, jnp.float32) * scale * factor_of
    return jnp.minimum(jnp.maximum(values, -most), most).astype(held_as)


def setup_inputs(seed: int = 0) -> dict:
    seeds = jax.random.split(jax.random.key(seed), 10)
    tracers = noise(seeds[0], (NTR, K, NJ, NI), 1.0, 6.0, ((2, 8), (3, 16)), jnp.float32)
    flow_east = jnp.clip(jax.random.uniform(seeds[1], (K, NJ, NI), jnp.float32, -0.35, 0.35) * steps_of(seeds[1], (K, NJ, NI), ((1, 8), (2, 16)), -0.4, 0.0), -0.35, 0.35)
    flow_north = jnp.clip(jax.random.uniform(seeds[2], (K, NJ, NI), jnp.float32, -0.35, 0.35) * steps_of(seeds[2], (K, NJ, NI), ((1, 8), (2, 16)), -0.4, 0.0), -0.35, 0.35)
    sea_mask = set_ends((jax.random.randint(seeds[3], (K, NJ, NI), 0, 8) < 7).astype(jnp.int32), jax.random.fold_in(seeds[3], 1), 0, 1)
    atm_fields = noise(seeds[4], (NF, NA), 1.0, 6.0, ((1, 128),))
    remap_weights = noise(seeds[5], (NW, CI, CI), CI ** -0.5, 0.5, ((0, 128),))
    remap_src = set_ends(jax.random.randint(seeds[6], (NW,), 0, ABLK_DEV), jax.random.fold_in(seeds[6], 1), 0, ABLK_DEV - 1).astype(jnp.int32)
    remap_dst = draw_remap_dst(jax.random.fold_in(seeds[9], 71), 0)
    fold_partner = draw_fold_partner(jax.random.fold_in(seeds[9], 71), 0)
    return {"tracers": tracers, "flow_east": flow_east, "flow_north": flow_north, "sea_mask": sea_mask, "atm_fields": atm_fields, "remap_weights": remap_weights, "remap_src": remap_src, "remap_dst": remap_dst, "fold_partner": fold_partner}


HEAT_SCALE = 0.1
FRESH_SCALE = 0.03
STRESS_SCALE = 0.02
HEAT_ALPHA_COEFF = 0.2
SALT_BETA_COEFF = 0.8
SLOPE_EPS = 0.5
DIFFUSIVITY = 0.1


def minmod(first, second):
    return 0.5 * (jnp.sign(first) + jnp.sign(second)) * jnp.minimum(jnp.abs(first), jnp.abs(second))


def vertical(field):
    upper = jnp.concatenate([field[1:], field[-1:]], 0)
    lower = jnp.concatenate([field[:1], field[:-1]], 0)
    return 0.5 * (upper - lower)


def mesh_layout(theta_tracer, saltiness_tracer, haloed_velocity, haloed_ocean_indicator, uppermost_indicator):
    given_latitudes = theta_tracer.shape[1] - 4
    given_longitudes = theta_tracer.shape[2] - 4
    seawater_mass_per_volume = SALT_BETA_COEFF * saltiness_tracer - HEAT_ALPHA_COEFF * theta_tracer
    density_dz = vertical(seawater_mass_per_volume)
    band_x = seawater_mass_per_volume[:, 2:given_latitudes + 2, 1:given_longitudes + 3]
    band_zx = density_dz[:, 2:given_latitudes + 2, 1:given_longitudes + 3]
    across_x = band_x[..., 1:] - band_x[..., :-1]
    strat_x = 0.5 * (band_zx[..., 1:] + band_zx[..., :-1])
    slope_x = across_x * strat_x / (strat_x * strat_x + SLOPE_EPS)
    band_y = seawater_mass_per_volume[:, 1:given_latitudes + 3, 2:given_longitudes + 2]
    band_zy = density_dz[:, 1:given_latitudes + 3, 2:given_longitudes + 2]
    across_y = band_y[:, 1:] - band_y[:, :-1]
    strat_y = 0.5 * (band_zy[:, 1:] + band_zy[:, :-1])
    slope_y = across_y * strat_y / (strat_y * strat_y + SLOPE_EPS)
    mask_x = haloed_ocean_indicator[:, 1:given_latitudes + 1, 0:given_longitudes + 1] * haloed_ocean_indicator[:, 1:given_latitudes + 1, 1:given_longitudes + 2]
    face_rows = jnp.arange(given_latitudes + 1)[None, :, None]
    above = jnp.where(uppermost_indicator & (face_rows == given_latitudes), 1.0, haloed_ocean_indicator[:, 1:given_latitudes + 2, 1:given_longitudes + 1])
    mask_y = haloed_ocean_indicator[:, 0:given_latitudes + 1, 1:given_longitudes + 1] * above
    flow_x = haloed_velocity[0][:, 1:given_latitudes + 1, 0:given_longitudes + 1] * mask_x
    flow_y = haloed_velocity[1][:, 0:given_latitudes + 1, 1:given_longitudes + 1] * mask_y
    slope_rows = jnp.arange(given_latitudes + 2)[:, None]
    keep_rows = 1.0 - jnp.where(uppermost_indicator & (slope_rows == given_latitudes + 1), 1.0, 0.0)
    return slope_x, slope_y, mask_x, mask_y, flow_x, flow_y, keep_rows


def advance(tracer_pad, geo):
    slope_x, slope_y, mask_x, mask_y, flow_x, flow_y, keep_rows = geo
    given_latitudes = tracer_pad.shape[1] - 4
    given_longitudes = tracer_pad.shape[2] - 4
    row_band = tracer_pad[:, 2:given_latitudes + 2, :]
    limited_x = minmod(row_band[..., 2:] - row_band[..., 1:-1], row_band[..., 1:-1] - row_band[..., :-2])
    cell_x = row_band[..., 1:-1]
    face_low = cell_x[..., :-1] + 0.5 * (1.0 - flow_x) * limited_x[..., :-1]
    face_high = cell_x[..., 1:] - 0.5 * (1.0 + flow_x) * limited_x[..., 1:]
    flux_x = flow_x * jnp.where(flow_x > 0, face_low, face_high)
    column_band = tracer_pad[:, :, 2:given_longitudes + 2]
    limited_y = minmod(column_band[:, 2:] - column_band[:, 1:-1], column_band[:, 1:-1] - column_band[:, :-2]) * keep_rows[None]
    cell_y = column_band[:, 1:-1]
    face_south = cell_y[:, :-1] + 0.5 * (1.0 - flow_y) * limited_y[:, :-1]
    face_north = cell_y[:, 1:] - 0.5 * (1.0 + flow_y) * limited_y[:, 1:]
    flux_y = flow_y * jnp.where(flow_y > 0, face_south, face_north)
    tracer_dz = vertical(tracer_pad)
    side_x = tracer_pad[:, 2:given_latitudes + 2, 1:given_longitudes + 3]
    side_zx = tracer_dz[:, 2:given_latitudes + 2, 1:given_longitudes + 3]
    iso_x = DIFFUSIVITY * mask_x * ((side_x[..., 1:] - side_x[..., :-1]) - slope_x * 0.5 * (side_zx[..., 1:] + side_zx[..., :-1]))
    side_y = tracer_pad[:, 1:given_latitudes + 3, 2:given_longitudes + 2]
    side_zy = tracer_dz[:, 1:given_latitudes + 3, 2:given_longitudes + 2]
    iso_y = DIFFUSIVITY * mask_y * ((side_y[:, 1:] - side_y[:, :-1]) - slope_y * 0.5 * (side_zy[:, 1:] + side_zy[:, :-1]))
    centre = tracer_pad[:, 2:given_latitudes + 2, 2:given_longitudes + 2]
    return (centre - (flux_x[..., 1:] - flux_x[..., :-1]) - (flux_y[:, 1:] - flux_y[:, :-1])
            + (iso_x[..., 1:] - iso_x[..., :-1]) + (iso_y[:, 1:] - iso_y[:, :-1]))


def apply_forcing(tracers, flow_east, flow_north, land_sea, forcing):
    heat, fresh, tau_x, tau_y = forcing[0], forcing[1], forcing[2], forcing[3]
    surface = tracers[:, 0]
    change = jnp.concatenate([HEAT_SCALE * heat[None], FRESH_SCALE * fresh[None] * surface[1:]], 0)
    forced = tracers.at[:, 0].set(surface + land_sea[0][None] * change)
    east = flow_east.at[0].add(STRESS_SCALE * tau_x)
    north = flow_north.at[0].add(STRESS_SCALE * tau_y)
    return forced, east, north


def pad_columns(field, width):
    return jnp.concatenate([field[..., -width:], field, field[..., :width]], -1)


def pad_rows(field, width):
    array_shape = list(field.shape)
    array_shape[-2] = width
    zeros = jnp.zeros(array_shape, field.dtype)
    return jnp.concatenate([zeros, field, zeros], -2)


def reference(tracers, flow_east, flow_north, sea_mask, atm_fields, remap_weights, remap_src, remap_dst, fold_partner):
    devices = N_LON * N_LAT
    atm_dev = atm_fields.reshape(NF, devices, ABLK_DEV, CI)
    weights_dev = remap_weights.reshape(devices, WB_DEV, CI, CI)
    source_dev = remap_src.reshape(devices, WB_DEV)
    target_dev = remap_dst.reshape(devices, WB_DEV)

    def add_device(total, index):
        blocks = atm_dev[:, index]
        picked = jnp.take(blocks, source_dev[index], axis=1).astype(jnp.float32)
        product = jnp.einsum('fwa,wca->wfc', picked, weights_dev[index].astype(jnp.float32))
        summed = jax.ops.segment_sum(product, target_dev[index], num_segments=NJ * N_LON)
        return total + summed, None

    total, _ = lax.scan(add_device, jnp.zeros((NJ * N_LON, NF, CI), jnp.float32), jnp.arange(devices))
    forcing = total.reshape(NJ, N_LON, NF, CI).transpose(2, 0, 1, 3).reshape(NF, NJ, NI)
    land_sea = sea_mask.astype(jnp.float32)
    forced, east, north = apply_forcing(tracers, flow_east, flow_north, land_sea, forcing)
    tracer_pad = pad_rows(pad_columns(forced, 2), 2)
    ghost = jnp.take(forced[:, :, NJ - 1, :], fold_partner, axis=2)
    tracer_pad = tracer_pad.at[:, :, NJ + 2, 2:NI + 2].set(ghost)
    haloed_velocity = pad_rows(pad_columns(jnp.stack([east, north]), 1), 1)
    haloed_ocean_indicator = pad_rows(pad_columns(land_sea, 1), 1)
    geo = mesh_layout(tracer_pad[0], tracer_pad[1], haloed_velocity, haloed_ocean_indicator, jnp.array(True))
    stepped = lax.map(lambda single: advance(single, geo), tracer_pad)
    tracers_next = stepped * haloed_ocean_indicator[None, :, 1:-1, 1:-1]
    return forcing, tracers_next
```

```python
import functools

import jax
import jax.numpy as jnp
from jax import lax
from jax.experimental import pallas as pl
from jax.experimental.pallas import tpu as pltpu
from jax.sharding import PartitionSpec as P

HEAT_SCALE = 0.1
FRESH_SCALE = 0.03
STRESS_SCALE = 0.02
HEAT_ALPHA_COEFF = 0.2
SALT_BETA_COEFF = 0.8
SLOPE_EPS = 0.5
DIFFUSIVITY = 0.1

NTR = 6
ROWS = 64
LANES = 128
GROUPS = 8
F32 = jnp.float32
VMEM_LIMIT = 56 * 1024 * 1024


def roll(x, shift):
    return pltpu.roll(x, shift % LANES, axis=1)


def lanes_of(shape):
    return lax.broadcasted_iota(jnp.int32, shape, len(shape) - 1)


def pack_kernel(tracers, east, north, mask, both_ref, cols_ref, up_ref, down_ref):
    lane_group = lanes_of((8, LANES)) // 4
    levels = east.shape[0]
    for k in range(levels):
        land = mask[k].astype(F32)
        fields = [tracers[t, k] for t in range(NTR)] + [east[k], land]
        for h in range(2):
            total = jnp.zeros((8, LANES), F32)
            for rr in range(4):
                start = (4 * h + rr) * 8
                for f in range(8):
                    moved = roll(fields[f][start : start + 8], 2 + 32 * rr + 4 * f)
                    total = jnp.where(lane_group == 8 * rr + f, moved, total)
            both_ref[k, h] = total
            cols_ref[k, h] = total
        fields[6] = north[k]
        for f in range(8):
            both_ref[k, 2, f : f + 1] = fields[f][ROWS - 1 : ROWS]
            for i in range(2):
                up_ref[k, i, f : f + 1] = fields[f][ROWS - 2 + i : ROWS - 1 + i]
                down_ref[k, i, f : f + 1] = fields[f][i : i + 1]


def pack_halos(tracers, east, north, mask):
    levels = east.shape[0]
    step = 2
    flow = pl.BlockSpec((step, ROWS, LANES), lambda i: (i, 0, 0))
    out = lambda n: pl.BlockSpec((step, n, 8, LANES), lambda i: (i, 0, 0, 0))
    shape = lambda n: jax.ShapeDtypeStruct((levels, n, 8, LANES), F32)
    return pl.pallas_call(
        pack_kernel,
        grid=(levels // step,),
        in_specs=[pl.BlockSpec((NTR, step, ROWS, LANES), lambda i: (0, i, 0, 0)), flow, flow, flow],
        out_specs=[out(3), out(2), out(2), out(2)],
        out_shape=[shape(3), shape(2), shape(2), shape(2)],
        compiler_params=pltpu.CompilerParams(vmem_limit_bytes=VMEM_LIMIT),
        name="pack_halos",
    )(tracers, east, north, mask)


def remap_kernel(n_lon, n_lat, per_step, src, dst, fold, atm, weights, out, blocks, edge, labels, count):
    step = pl.program_id(0)
    devices = n_lon * n_lat

    @pl.when(step == 0)
    def _():
        blocks[...] = jnp.zeros_like(blocks)
        wide = atm[...].astype(F32)
        for b in range(blocks.shape[0]):
            blocks[b, 0:4] = wide[:, b * LANES : (b + 1) * LANES]
        out[...] = jnp.zeros_like(out)
        edge[...] = jnp.zeros_like(edge)
        labels[...] = jnp.zeros_like(labels)

        def clear(i, _):
            count[i] = 0
            return 0

        lax.fori_loop(0, devices, clear, 0)

    lane1 = lanes_of((1, LANES))

    def one(j, _):
        w = step * per_step + j
        place = dst[w]
        lon = place % n_lon
        row = place // n_lon
        local = row % ROWS
        owner = lon * n_lat + row // ROWS
        slot = count[owner]
        count[owner] = slot + 1
        left = blocks[src[w]].astype(jnp.bfloat16)
        product = lax.dot_general(left, weights[j], (((1,), (1,)), ((), ())), preferred_element_type=F32)[0:4]
        out[owner * GROUPS + slot] = product
        labels[pl.ds(owner, 1)] = jnp.where(lane1 == slot, (local + 1).astype(F32), labels[pl.ds(owner, 1)])
        kind = jnp.where(local < 2, local, local - (ROWS - 4))
        is_edge = jnp.logical_or(local < 2, local >= ROWS - 2)
        at = jnp.where(is_edge, owner * 4 + kind, devices * 4)
        edge[at] = edge[at] + product
        return 0

    lax.fori_loop(0, per_step, one, 0, unroll=8)

    @pl.when(step == pl.num_programs(0) - 1)
    def _():
        lane4 = lanes_of((4, LANES))
        high = fold[0] // LANES
        low = fold[0] % LANES
        l_iota = lax.broadcasted_iota(jnp.int32, (LANES, LANES), 0)
        i_iota = lax.broadcasted_iota(jnp.int32, (LANES, LANES), 1)
        reverse = (l_iota == (low - i_iota + LANES) % LANES).astype(F32)
        strips = []
        for p in range(n_lon):
            first = edge[(((high - p + 2 * n_lon) % n_lon) * n_lat + n_lat - 1) * 4 + 3]
            second = edge[(((high - p - 1 + 2 * n_lon) % n_lon) * n_lat + n_lat - 1) * 4 + 3]
            strips.append(jnp.where(lane4 <= low, first, second))
        ghost = jnp.dot(
            jnp.concatenate(strips, 0), reverse, precision=lax.Precision.HIGHEST, preferred_element_type=F32
        )
        packed = []
        for owner in range(devices):
            total = jnp.zeros((4, LANES), F32)
            for n in range(4):
                moved = roll(out[owner * GROUPS + n], 2 + 4 * n)
                total = jnp.where(lane4 // 4 == n, moved, total)
            out[owner * GROUPS + 5] = total
        own = labels[...]
        lane = lanes_of(own.shape)
        west = jnp.concatenate([own[devices - n_lat :], own[: devices - n_lat]], 0)
        east = jnp.concatenate([own[n_lat:], own[:n_lat]], 0)
        both = jnp.where(lane < 4, own, jnp.where(lane < 8, roll(west, 4), roll(east, 8)))
        labels[...] = both
        for lat in range(n_lat):
            packs = [out[(lon * n_lat + lat) * GROUPS + 5] for lon in range(n_lon)]
            for lon in range(n_lon):
                owner = lon * n_lat + lat
                base = owner * GROUPS
                out[base + 4, 0:1] = labels[owner : owner + 1]
                from_west = packs[(lon - 1) % n_lon]
                from_east = packs[(lon + 1) % n_lon]
                out[base + 5] = jnp.where(lane4 < 16, from_west, roll(from_east, 16))
                if lat < n_lat - 1:
                    above = (owner + 1) * 4
                    out[base + 6, 0:2] = edge[above, 0:2]
                    out[base + 6, 2:4] = edge[above + 1, 0:2]
                else:
                    out[base + 6, 0:2] = ghost[4 * lon : 4 * lon + 2]
                    out[base + 6, 2:4] = ghost[4 * lon : 4 * lon + 2]
                if lat > 0:
                    below = (owner - 1) * 4
                    out[base + 7, 0:2] = edge[below + 3, 0:2]
                    out[base + 7, 2:4] = edge[below + 2, 0:2]
                    out[base + 4, 1:2] = edge[below + 3, 3:4]


def remap(atm, weights, src, dst, fold_c, n_lon, n_lat):
    sends = weights.shape[0]
    devices = n_lon * n_lat
    per_step = 32
    blocks = atm.shape[1] // LANES
    return pl.pallas_call(
        functools.partial(remap_kernel, n_lon, n_lat, per_step),
        grid=(sends // per_step,),
        in_specs=[
            pl.BlockSpec(memory_space=pltpu.SMEM),
            pl.BlockSpec(memory_space=pltpu.SMEM),
            pl.BlockSpec(memory_space=pltpu.SMEM),
            pl.BlockSpec(atm.shape, lambda i: (0, 0)),
            pl.BlockSpec((per_step, LANES, LANES), lambda i: (i, 0, 0)),
        ],
        out_specs=pl.BlockSpec((devices * GROUPS, 4, LANES), lambda i: (0, 0, 0)),
        out_shape=jax.ShapeDtypeStruct((devices * GROUPS, 4, LANES), F32),
        scratch_shapes=[
            pltpu.VMEM((blocks, 8, LANES), F32),
            pltpu.VMEM((devices * 4 + 1, 4, LANES), F32),
            pltpu.VMEM((devices, LANES), F32),
            pltpu.SMEM((devices,), jnp.int32),
        ],
        compiler_params=pltpu.CompilerParams(vmem_limit_bytes=VMEM_LIMIT),
        name="remap",
    )(src, dst, fold_c, atm, weights)


def minmod(a, b):
    return jnp.maximum(jnp.minimum(a, b), jnp.minimum(jnp.maximum(a, b), 0.0))


def face_coefficients(flow, mask, drho, zrho):
    diff = DIFFUSIVITY * mask
    strat = 0.25 * zrho
    slope = drho * strat / (strat * strat + SLOPE_EPS)
    up = jnp.maximum(flow, 0.0)
    down = jnp.minimum(flow, 0.0)
    return (
        up + diff,
        down - diff,
        0.5 * up * (1.0 - up),
        -0.5 * down * (1.0 + down),
        0.25 * diff * slope,
    )


def density(temperature, salinity):
    return SALT_BETA_COEFF * salinity - HEAT_ALPHA_COEFF * temperature


def spread(x, lane32):
    for width in (4, 8, 16):
        x = jnp.where(lane32 < width, x, roll(x, width))
    return x


def edge_values(halo, own, lane32):
    hm, h0, hp = halo
    om, o0, op = own
    zh, zo = hp - hm, op - om
    west, first = roll(h0, -1), roll(o0, -2)
    d_west = first - west
    s_west = minmod(d_west, west - h0)
    s_first = minmod(roll(o0, -3) - first, d_west)
    z_west = roll(zh, -1) + roll(zo, -2)
    beyond = roll(h0, -2)
    s_beyond = minmod(roll(h0, -3) - beyond, beyond - roll(o0, -1))
    z_beyond = roll(zh, -2)
    mask = roll(west, -28) * roll(first, -28)
    flow = roll(west, -24) * mask
    coefs = face_coefficients(
        flow, mask, density(d_west, roll(d_west, -4)), density(z_west, roll(z_west, -4))
    )
    a, b, p, q, v = [spread(x, lane32) for x in coefs]
    flux = a * west + b * first + p * s_west + q * s_first + v * z_west
    return beyond, z_beyond, s_beyond, d_west, flux


def level_step(tracer, rows_below, rows_above, halo, own, east, north, land, write, scratch):
    cpad, zpad, spad, fpad, mpad, npad = scratch
    lane8 = lanes_of((8, LANES))
    first_lane = lanes_of((ROWS, LANES)) == 0
    for t in range(NTR):
        cpad[t, 8:72] = tracer(0, t)
        zpad[t, 8:72] = tracer(1, t) - tracer(-1, t)
        for i in range(2):
            cpad[t, 6 + i : 7 + i] = rows_below(0, i, t)
            cpad[t, 72 + i : 73 + i] = rows_above(0, i, t)
        zpad[t, 7:8] = rows_below(1, 1, t) - rows_below(-1, 1, t)
        zpad[t, 72:73] = rows_above(1, 0, t) - rows_above(-1, 0, t)
    mpad[8:72] = land
    mpad[7:8] = rows_below(0, 1, 7)
    mpad[72:73] = rows_above(0, 0, 7)
    npad[8:72] = north
    npad[7:8] = rows_below(0, 1, 6)

    edges = [
        edge_values([halo(j, h) for j in (-1, 0, 1)], [own(j, h) for j in (-1, 0, 1)], lane8 % 32)
        for h in range(2)
    ]

    def at_first(which, f):
        return jnp.concatenate([roll(edges[r // 4][which], -(32 * (r % 4) + 4 * f)) for r in range(8)], 0)

    def eastward(x, which, f):
        return roll(jnp.where(first_lane, at_first(which, f), x), -1)

    def x_parts(t):
        c = cpad[t, 8:72]
        z = zpad[t, 8:72]
        c_east = eastward(c, 0, t)
        return c, c_east, z + eastward(z, 1, t)

    def y_parts(t):
        c = cpad[t, 7:79]
        return c, cpad[t, 8:80], zpad[t, 7:79] + zpad[t, 8:80]

    xs = [x_parts(t) for t in range(2)]
    ys = [y_parts(t) for t in range(2)]
    mask_x = land * eastward(land, 0, 7)
    ax, bx, px, qx, vx = face_coefficients(
        east * mask_x, mask_x, density(xs[0][1] - xs[0][0], xs[1][1] - xs[1][0]), density(xs[0][2], xs[1][2])
    )
    mask_y = mpad[7:79] * mpad[8:80]
    ay, by, py, qy, vy = face_coefficients(
        npad[7:79] * mask_y, mask_y, density(ys[0][1] - ys[0][0], ys[1][1] - ys[1][0]), density(ys[0][2], ys[1][2])
    )
    for t in range(NTR):
        c, c_east, z = xs[t] if t < 2 else x_parts(t)
        d = c_east - c
        s = minmod(d, jnp.where(first_lane, at_first(3, t), roll(d, 1)))
        flux = ax * c + bx * c_east + px * s + qx * eastward(s, 2, t) + vx * z
        result = c - (flux - jnp.where(first_lane, at_first(4, t), roll(flux, 1)))
        c, c_north, z = ys[t] if t < 2 else y_parts(t)
        s = minmod(c_north - c, c - cpad[t, 6:78])
        spad[0:72] = s
        flux = ay * c + by * c_north + py * s + qy * spad[1:73] + vy * z
        fpad[0:72] = flux
        write(t, land * (result - (fpad[1:65] - fpad[0:64])))


def level_scratch():
    return [
        pltpu.VMEM((NTR, 80, LANES), F32),
        pltpu.VMEM((NTR, 80, LANES), F32),
        pltpu.VMEM((80, LANES), F32),
        pltpu.VMEM((80, LANES), F32),
        pltpu.VMEM((80, LANES), F32),
        pltpu.VMEM((80, LANES), F32),
    ]


def deep_kernel(first, below, here, above, east, north, mask, west_cols, east_cols, own_cols, row_below, row_above, out, *scratch):
    k = pl.program_id(0) + first
    levels = own_cols.shape[0]
    level = {-1: k - 1, 0: k, 1: jnp.minimum(k + 1, levels - 1)}
    lane_of_four = lanes_of((8, LANES)) % 4
    sources = {-1: below, 0: here, 1: above}

    def write(t, value):
        out[t, 0] = value

    level_step(
        lambda j, t: sources[j][t, 0],
        lambda j, i, f: row_below[level[j], i, f : f + 1],
        lambda j, i, f: row_above[level[j], i, f : f + 1],
        lambda j, h: jnp.where(lane_of_four < 2, west_cols[level[j], h], east_cols[level[j], h]),
        lambda j, h: own_cols[level[j], h],
        east[0],
        north[0],
        mask[0].astype(F32),
        write,
        scratch,
    )


def deep_levels(first, tracers, east, north, mask, west_cols, east_cols, own_cols, row_below, row_above):
    levels = tracers.shape[1]
    block = (NTR, 1, ROWS, LANES)
    flow = pl.BlockSpec((1, ROWS, LANES), lambda i: (i + first, 0, 0))
    whole = lambda x: pl.BlockSpec(x.shape, lambda i: (0,) * x.ndim)
    return pl.pallas_call(
        functools.partial(deep_kernel, first),
        grid=(levels - first,),
        in_specs=[
            pl.BlockSpec(block, lambda i: (0, i + first - 1, 0, 0)),
            pl.BlockSpec(block, lambda i: (0, i + first, 0, 0)),
            pl.BlockSpec(block, lambda i: (0, jnp.minimum(i + first + 1, levels - 1), 0, 0)),
            flow,
            flow,
            flow,
        ]
        + [whole(x) for x in (west_cols, east_cols, own_cols, row_below, row_above)],
        out_specs=pl.BlockSpec(block, lambda i: (0, i + first, 0, 0)),
        out_shape=jax.ShapeDtypeStruct(tracers.shape, F32),
        scratch_shapes=level_scratch(),
        compiler_params=pltpu.CompilerParams(vmem_limit_bytes=VMEM_LIMIT),
        name="deep_levels",
    )(tracers, tracers, tracers, east, north, mask, west_cols, east_cols, own_cols, row_below, row_above)


def expand(x, lane):
    total = x
    for f in range(2, 6):
        total = jnp.where(lane // 4 == f, roll(x, 4 * (f - 1)), total)
    return jnp.where(lane // 4 == 6, roll(x, 16), total)


def pack_rows(tiles, lane):
    packed = []
    for h in range(2):
        total = jnp.zeros((8, LANES), F32)
        for rr in range(4):
            total = jnp.where(lane // 32 == rr, roll(tiles[4 * h + rr], 32 * rr), total)
        packed.append(total)
    return packed


def force_columns(cols, force, lane):
    field = (lane % 32) // 4
    mask = spread(roll(cols, -28), lane % 32)
    tracer_change = mask * (force * jnp.where(field == 0, HEAT_SCALE, FRESH_SCALE * cols))
    return cols + jnp.where(field < 6, tracer_change, jnp.where(field == 6, STRESS_SCALE * force, 0.0))


def force_rows(rows, mask, heat, fresh, tau):
    field = lax.broadcasted_iota(jnp.int32, (8, LANES), 0)
    tracer_change = mask * jnp.where(field == 0, HEAT_SCALE * heat, FRESH_SCALE * fresh * rows)
    return rows + jnp.where(field < 6, tracer_change, jnp.where(field == 6, STRESS_SCALE * tau, 0.0))


def surface_kernel(
    top, arrived, tracers, east, north, mask, west_cols, east_cols, own_cols, row_below, row_above, _, forcing, out,
    forced, rows_b, rows_a, cols_h, cols_o, *scratch
):
    devices = arrived.shape[0] // (4 * GROUPS)
    stride = 4 * GROUPS
    lane = lanes_of((8, LANES))
    lane_of_four = lane % 4

    def gathered(group, row):
        return arrived[pl.ds(4 * group + row, devices, stride=stride), :]

    labels = gathered(4, 0).T
    row_id = lax.broadcasted_iota(jnp.int32, (ROWS, devices), 0).astype(F32) + 1.0

    def pick(n):
        return (labels[n : n + 1] == row_id).astype(F32)

    def dot(a, b):
        return jnp.dot(a, b, precision=lax.Precision.HIGHEST, preferred_element_type=F32)

    flux = jnp.zeros((ROWS, 4 * LANES), F32)
    for n in range(4):
        flux += dot(pick(n), jnp.concatenate([gathered(n, f) for f in range(4)], 1))
    fields = [flux[:, LANES * f : LANES * (f + 1)] for f in range(4)]
    for f in range(4):
        forcing[f] = fields[f]
    heat, fresh, tau_x, tau_y = fields

    wide = lanes_of((devices, LANES))
    sides = [gathered(5, f) for f in range(3)]
    beside = jnp.zeros((ROWS, LANES), F32)
    for side in range(2):
        for n in range(4):
            back = -4 * n - 16 * side
            lined = jnp.where(
                wide < 4, roll(sides[0], back), jnp.where(wide < 8, roll(sides[1], back + 4), roll(sides[2], back + 8))
            )
            lined = jnp.where((wide < 12) & (wide % 4 // 2 == side), lined, 0.0)
            beside += dot(pick(4 + 4 * side + n), lined)

    def summed(group):
        return jnp.sum(arrived[...].reshape(devices, GROUPS, 4, LANES)[:, group], 0)

    over = [jnp.sum(gathered(6, f), 0, keepdims=True) for f in range(4)]
    under = [jnp.sum(gathered(7, f), 0, keepdims=True) for f in range(4)]
    tau_under = jnp.sum(gathered(4, 1), 0, keepdims=True)

    land = [mask[k].astype(F32) for k in range(2)]
    forced[0] = tracers[0, 0] + land[0] * (HEAT_SCALE * heat)
    for t in range(1, NTR):
        c = tracers[t, 0]
        forced[t] = c + land[0] * (FRESH_SCALE * fresh * c)
    rows_b[0] = force_rows(row_below[0, 0], row_below[0, 0, 7:8], under[2], under[3], 0.0)
    rows_b[1] = force_rows(row_below[0, 1], row_below[0, 1, 7:8], under[0], under[1], tau_under)
    near = jnp.where(top[0] > 0, row_above[0, 1, 7:8], row_above[0, 0, 7:8])
    rows_a[0] = force_rows(row_above[0, 0], near, over[0], over[1], 0.0)
    rows_a[1] = force_rows(row_above[0, 1], row_above[0, 1, 7:8], over[2], over[3], 0.0)
    own_tiles, halo_tiles = [], []
    for r in range(8):
        part = slice(8 * r, 8 * r + 8)
        mine = jnp.where(lane < 4, roll(heat[part], 2), jnp.where(lane < 8, roll(fresh[part], 6), roll(tau_x[part], 10)))
        own_tiles.append(expand(mine, lane))
        halo_tiles.append(expand(beside[part], lane))
    own_force, halo_force = pack_rows(own_tiles, lane), pack_rows(halo_tiles, lane)
    for h in range(2):
        cols = jnp.where(lane_of_four < 2, west_cols[0, h], east_cols[0, h])
        cols_h[h] = force_columns(cols, halo_force[h], lane)
        cols_o[h] = force_columns(own_cols[0, h], own_force[h], lane)

    for k in range(2):

        def at(j):
            return max(k + j, 0)

        def write(t, value):
            out[t, k] = value

        def plain_halo(level, h):
            return jnp.where(lane_of_four < 2, west_cols[level, h], east_cols[level, h])

        level_step(
            lambda j, t: forced[t] if at(j) == 0 else tracers[t, at(j)],
            lambda j, i, f: rows_b[i, f : f + 1] if at(j) == 0 else row_below[at(j), i, f : f + 1],
            lambda j, i, f: rows_a[i, f : f + 1] if at(j) == 0 else row_above[at(j), i, f : f + 1],
            lambda j, h: cols_h[h] if at(j) == 0 else plain_halo(at(j), h),
            lambda j, h: cols_o[h] if at(j) == 0 else own_cols[at(j), h],
            east[k] + STRESS_SCALE * tau_x if k == 0 else east[k],
            north[k] + STRESS_SCALE * tau_y if k == 0 else north[k],
            land[k],
            write,
            scratch,
        )


def surface_levels(top, arrived, tracers, east, north, mask, west_cols, east_cols, own_cols, row_below, row_above, done):
    block = lambda n: pl.BlockSpec((NTR, n, ROWS, LANES), lambda i: (0, 0, 0, 0))
    flow = pl.BlockSpec((2, ROWS, LANES), lambda i: (0, 0, 0))
    halo = lambda x: pl.BlockSpec((3,) + x.shape[1:], lambda i: (0, 0, 0, 0))
    return pl.pallas_call(
        surface_kernel,
        grid=(1,),
        in_specs=[
            pl.BlockSpec(memory_space=pltpu.SMEM),
            pl.BlockSpec(arrived.shape, lambda i: (0, 0)),
            block(3),
            flow,
            flow,
            flow,
        ]
        + [halo(x) for x in (west_cols, east_cols, own_cols, row_below, row_above)]
        + [pl.BlockSpec(memory_space=pl.ANY)],
        out_specs=[pl.BlockSpec((4, ROWS, LANES), lambda i: (0, 0, 0)), block(2)],
        out_shape=[jax.ShapeDtypeStruct((4, ROWS, LANES), F32), jax.ShapeDtypeStruct(tracers.shape, F32)],
        input_output_aliases={11: 1},
        scratch_shapes=[
            pltpu.VMEM((NTR, ROWS, LANES), F32),
            pltpu.VMEM((2, 8, LANES), F32),
            pltpu.VMEM((2, 8, LANES), F32),
            pltpu.VMEM((2, 8, LANES), F32),
            pltpu.VMEM((2, 8, LANES), F32),
        ]
        + level_scratch(),
        compiler_params=pltpu.CompilerParams(vmem_limit_bytes=VMEM_LIMIT),
        name="surface_levels",
    )(top, arrived, tracers, east, north, mask, west_cols, east_cols, own_cols, row_below, row_above, done)


def fold_ghost(own_top, west_top, c, n_lon, n_lat):
    low = c % LANES
    lane = jnp.arange(LANES)
    joined = jnp.where(lane <= low, own_top, west_top)
    reverse = (lane[:, None] == (low - lane[None, :]) % LANES).astype(F32)
    strip = jnp.einsum("kfl,li->kfi", joined, reverse, precision=lax.Precision.HIGHEST, preferred_element_type=F32)

    def move(b):
        pairs = [(q * n_lat + n_lat - 1, ((b - q) % n_lon) * n_lat + n_lat - 1) for q in range(n_lon)]
        return lambda x: lax.ppermute(x, ("lon", "lat"), pairs)

    return lax.switch(c // LANES, [move(b) for b in range(n_lon)], strip)


def body(tracers, flow_east, flow_north, sea_mask, atm_fields, remap_weights, remap_src, remap_dst, fold_partner):
    n_lon, n_lat = lax.axis_size("lon"), lax.axis_size("lat")
    devices = n_lon * n_lat
    lon, lat = lax.axis_index("lon"), lax.axis_index("lat")
    columns = n_lon * LANES
    c = (fold_partner[0] + lon * LANES) % columns

    outgoing = remap(atm_fields, remap_weights, remap_src, remap_dst, c[None], n_lon, n_lat)
    arrived = lax.all_to_all(
        outgoing.reshape(devices, 4 * GROUPS, LANES), ("lon", "lat"), split_axis=0, concat_axis=0, tiled=True
    )

    both, own_cols, up, down = pack_halos(tracers, flow_east, flow_north, sea_mask)
    right = [(i, (i + 1) % n_lon) for i in range(n_lon)]
    left = [(j, i) for i, j in right]
    north = [(i, i + 1) for i in range(n_lat - 1)]
    south = [(j, i) for i, j in north]
    west_cols = lax.ppermute(both, "lon", right)
    east_cols = lax.ppermute(own_cols, "lon", left)
    row_below = lax.ppermute(up, "lat", north)
    row_above = lax.ppermute(down, "lat", south)
    ghost = fold_ghost(both[:, 2], west_cols[:, 2], c, n_lon, n_lat)
    is_top = lat == n_lat - 1
    field = jnp.arange(8)[:, None]
    ghost_rows = jnp.stack([jnp.where(field == 7, 1.0, ghost), ghost], 1)
    row_above = jnp.where(is_top, ghost_rows, row_above)
    halos = (west_cols, east_cols, own_cols, row_below, row_above)

    done = deep_levels(2, tracers, flow_east, flow_north, sea_mask, *halos)
    top = is_top.astype(jnp.int32)[None]
    return surface_levels(
        top, arrived.reshape(devices * 4 * GROUPS, LANES), tracers, flow_east, flow_north, sea_mask, *halos, done
    )


def solution(mesh):
    placed = (
        P(None, None, "lat", "lon"),
        P(None, "lat", "lon"),
        P(None, "lat", "lon"),
        P(None, "lat", "lon"),
        P(None, ("lon", "lat")),
        P(("lon", "lat"), None, None),
        P(("lon", "lat")),
        P(("lon", "lat")),
        P("lon"),
    )
    return jax.shard_map(
        body,
        mesh=mesh,
        in_specs=placed,
        out_specs=(P(None, "lat", "lon"), P(None, None, "lat", "lon")),
        check_vma=False,
    )
```

```python
import functools

import jax
import jax.numpy as jnp
from jax import lax
from jax.experimental import pallas as pl
from jax.experimental.pallas import tpu as pltpu
from jax.sharding import PartitionSpec as P

HEAT_SCALE = 0.1
FRESH_SCALE = 0.03
STRESS_SCALE = 0.02
HEAT_ALPHA_COEFF = 0.2
SALT_BETA_COEFF = 0.8
SLOPE_EPS = 0.5
DIFFUSIVITY = 0.1

NTR = 6
ROWS = 64
LANES = 128
GROUPS = 8
F32 = jnp.float32
TOGETHER = 2
EDGE_LEVELS = 8
VMEM_LIMIT = 56 * 1024 * 1024


def roll(x, shift):
    return pltpu.roll(x, shift % LANES, axis=1)


def lanes_of(shape):
    return lax.broadcasted_iota(jnp.int32, shape, len(shape) - 1)


def pack_kernel(tracers, east, north, mask, both_ref, cols_ref, up_ref, down_ref):
    lane_group = lanes_of((8, LANES)) // 4
    levels = east.shape[0]
    def one(k, _):
        land = mask[k].astype(F32)
        for h in range(2):
            total = jnp.zeros((8, LANES), F32)
            for rr in range(4):
                start = (4 * h + rr) * 8
                for f in range(8):
                    if f < NTR:
                        tile = tracers[f, k, start : start + 8]
                    else:
                        tile = land[start : start + 8] if f == 7 else east[k, start : start + 8]
                    moved = roll(tile, 2 + 32 * rr + 4 * f)
                    total = jnp.where(lane_group == 8 * rr + f, moved, total)
            both_ref[k, h] = total
            cols_ref[k, h] = total

        def row(f, r):
            if f < NTR:
                return tracers[f, k, r : r + 1]
            return land[r : r + 1] if f == 7 else north[k, r : r + 1]

        for f in range(8):
            both_ref[k, 2, f : f + 1] = row(f, ROWS - 1)
            for i in range(2):
                up_ref[k, i, f : f + 1] = row(f, ROWS - 2 + i)
                down_ref[k, i, f : f + 1] = row(f, i)
        return 0

    lax.fori_loop(0, levels, one, 0)


def pack_halos(tracers, east, north, mask):
    levels = east.shape[0]
    step = 6
    flow = pl.BlockSpec((step, ROWS, LANES), lambda i: (i, 0, 0))
    out = lambda n: pl.BlockSpec((step, n, 8, LANES), lambda i: (i, 0, 0, 0))
    shape = lambda n: jax.ShapeDtypeStruct((levels, n, 8, LANES), F32)
    return pl.pallas_call(
        pack_kernel,
        grid=(levels // step,),
        in_specs=[pl.BlockSpec((NTR, step, ROWS, LANES), lambda i: (0, i, 0, 0)), flow, flow, flow],
        out_specs=[out(3), out(2), out(2), out(2)],
        out_shape=[shape(3), shape(2), shape(2), shape(2)],
        compiler_params=pltpu.CompilerParams(vmem_limit_bytes=VMEM_LIMIT),
        name="pack_halos",
    )(tracers, east, north, mask)


def remap_kernel(n_lon, n_lat, per_step, src, dst, fold, atm, weights, out, blocks, edge, labels, count):
    step = pl.program_id(0)
    devices = n_lon * n_lat

    @pl.when(step == 0)
    def _():
        blocks[...] = jnp.zeros_like(blocks)
        wide = atm[...].astype(F32)
        for b in range(blocks.shape[0]):
            blocks[b, 0:4] = wide[:, b * LANES : (b + 1) * LANES]
        out[...] = jnp.zeros_like(out)
        edge[...] = jnp.zeros_like(edge)
        labels[...] = jnp.zeros_like(labels)

        def clear(i, _):
            count[i] = 0
            return 0

        lax.fori_loop(0, devices, clear, 0)

    lane1 = lanes_of((1, LANES))
    batch = 8

    def several(i, _):
        places, lefts = [], []
        for j in range(batch):
            w = step * per_step + batch * i + j
            place = dst[w]
            lon = place & (n_lon - 1) if n_lon & (n_lon - 1) == 0 else place % n_lon
            row = place // n_lon
            local = row % ROWS
            owner = lon * n_lat + row // ROWS
            slot = count[owner]
            count[owner] = slot + 1
            kind = jnp.where(local < 2, local, local - (ROWS - 4))
            is_edge = jnp.logical_or(local < 2, local >= ROWS - 2)
            places.append((owner, slot, local, jnp.where(is_edge, owner * 4 + kind, devices * 4)))
            lefts.append(blocks[src[w], 0:4])
        left = jnp.concatenate(lefts, 0).astype(jnp.bfloat16)
        right = weights[pl.ds(pl.multiple_of(batch * i, batch), batch)].reshape(batch * LANES, LANES)
        products = lax.dot_general(left, right, (((1,), (1,)), ((), ())), preferred_element_type=F32)
        for j, (owner, slot, local, at) in enumerate(places):
            product = products[4 * j : 4 * j + 4, LANES * j : LANES * (j + 1)]
            out[owner * GROUPS + slot] = product
            labels[pl.ds(owner, 1)] = jnp.where(lane1 == slot, (local + 1).astype(F32), labels[pl.ds(owner, 1)])
            edge[at] = edge[at] + product
        return 0

    lax.fori_loop(0, per_step // batch, several, 0, unroll=2)

    @pl.when(step == pl.num_programs(0) - 1)
    def _():
        lane4 = lanes_of((4, LANES))
        high = fold[0] // LANES
        low = fold[0] % LANES
        l_iota = lax.broadcasted_iota(jnp.int32, (LANES, LANES), 0)
        i_iota = lax.broadcasted_iota(jnp.int32, (LANES, LANES), 1)
        reverse = (l_iota == (low - i_iota + LANES) % LANES).astype(F32)
        strips = []
        for p in range(n_lon):
            first = edge[(((high - p + 2 * n_lon) % n_lon) * n_lat + n_lat - 1) * 4 + 3]
            second = edge[(((high - p - 1 + 2 * n_lon) % n_lon) * n_lat + n_lat - 1) * 4 + 3]
            strips.append(jnp.where(lane4 <= low, first, second))
        ghost = jnp.dot(
            jnp.concatenate(strips, 0), reverse, precision=lax.Precision.HIGHEST, preferred_element_type=F32
        )
        packed = []
        for owner in range(devices):
            total = jnp.zeros((4, LANES), F32)
            for n in range(4):
                moved = roll(out[owner * GROUPS + n], 2 + 4 * n)
                total = jnp.where(lane4 // 4 == n, moved, total)
            out[owner * GROUPS + 5] = total
        own = labels[...]
        lane = lanes_of(own.shape)
        west = jnp.concatenate([own[devices - n_lat :], own[: devices - n_lat]], 0)
        east = jnp.concatenate([own[n_lat:], own[:n_lat]], 0)
        both = jnp.where(lane < 4, own, jnp.where(lane < 8, roll(west, 4), roll(east, 8)))
        labels[...] = both
        for lat in range(n_lat):
            packs = [out[(lon * n_lat + lat) * GROUPS + 5] for lon in range(n_lon)]
            for lon in range(n_lon):
                owner = lon * n_lat + lat
                base = owner * GROUPS
                out[base + 4, 0:1] = labels[owner : owner + 1]
                from_west = packs[(lon - 1) % n_lon]
                from_east = packs[(lon + 1) % n_lon]
                out[base + 5] = jnp.where(lane4 < 16, from_west, roll(from_east, 16))
                if lat < n_lat - 1:
                    above = (owner + 1) * 4
                    out[base + 6, 0:2] = edge[above, 0:2]
                    out[base + 6, 2:4] = edge[above + 1, 0:2]
                else:
                    out[base + 6, 0:2] = ghost[4 * lon : 4 * lon + 2]
                    out[base + 6, 2:4] = ghost[4 * lon : 4 * lon + 2]
                if lat > 0:
                    below = (owner - 1) * 4
                    out[base + 7, 0:2] = edge[below + 3, 0:2]
                    out[base + 7, 2:4] = edge[below + 2, 0:2]
                    out[base + 4, 1:2] = edge[below + 3, 3:4]


def remap(atm, weights, src, dst, fold_c, n_lon, n_lat):
    sends = weights.shape[0]
    devices = n_lon * n_lat
    per_step = 32
    blocks = atm.shape[1] // LANES
    return pl.pallas_call(
        functools.partial(remap_kernel, n_lon, n_lat, per_step),
        grid=(sends // per_step,),
        in_specs=[
            pl.BlockSpec(memory_space=pltpu.SMEM),
            pl.BlockSpec(memory_space=pltpu.SMEM),
            pl.BlockSpec(memory_space=pltpu.SMEM),
            pl.BlockSpec(atm.shape, lambda i: (0, 0)),
            pl.BlockSpec((per_step, LANES, LANES), lambda i: (i, 0, 0)),
        ],
        out_specs=pl.BlockSpec((devices * GROUPS, 4, LANES), lambda i: (0, 0, 0)),
        out_shape=jax.ShapeDtypeStruct((devices * GROUPS, 4, LANES), F32),
        scratch_shapes=[
            pltpu.VMEM((blocks, 8, LANES), F32),
            pltpu.VMEM((devices * 4 + 1, 4, LANES), F32),
            pltpu.VMEM((devices, LANES), F32),
            pltpu.SMEM((devices,), jnp.int32),
        ],
        compiler_params=pltpu.CompilerParams(vmem_limit_bytes=VMEM_LIMIT),
        name="remap",
    )(src, dst, fold_c, atm, weights)


def minmod(a, b):
    return jnp.maximum(jnp.minimum(a, b), jnp.minimum(jnp.maximum(a, b), 0.0))


def face_coefficients(flow, mask, drho, zrho):
    diff = DIFFUSIVITY * mask
    strat = 0.25 * zrho
    slope = drho * strat / (strat * strat + SLOPE_EPS)
    up = jnp.maximum(flow, 0.0)
    down = jnp.minimum(flow, 0.0)
    return (
        up + diff,
        down - diff,
        0.5 * up * (1.0 - up),
        -0.5 * down * (1.0 + down),
        0.25 * diff * slope,
    )


def density(temperature, salinity):
    return SALT_BETA_COEFF * salinity - HEAT_ALPHA_COEFF * temperature


def spread(x, lane32):
    for width in (4, 8, 16):
        x = jnp.where(lane32 < width, x, roll(x, width))
    return x


def edge_values(halo, own):
    lane = lanes_of(halo(0, 0).shape)
    lane4, lane32 = lane % 4, lane % 32
    east = lane4 == 0
    parts = []
    for h in range(2):
        p, o = halo(0, h), own(0, h)
        zp, zo = halo(1, h) - halo(-1, h), own(1, h) - own(-1, h)
        o1, p2, zp2 = roll(o, -1), roll(p, -2), roll(zp, -2)
        zo1 = roll(zo, -1)
        parts.append(
            (
                jnp.where(east, o, roll(p, 1)),
                jnp.where(east, o1, p),
                jnp.where(east, p2, o1),
                jnp.where(east, roll(p, -3), roll(o, -2)),
                jnp.where(east, zo1, zp),
                jnp.where(east, zp2, zo1),
            )
        )
    c0, c1, c2, c3, z1, z2 = [jnp.where(lane4 < 2, x, roll(y, 2)) for x, y in zip(*parts)]
    d2 = c2 - c1
    s1, s2 = minmod(d2, c1 - c0), minmod(c3 - c2, d2)
    z = z1 + z2
    mask = roll(c1 * c2, -28)
    coefs = face_coefficients(roll(c1, -24) * mask, mask, density(d2, roll(d2, -4)), density(z, roll(z, -4)))
    a, b, p, q, v = [spread(x, lane32) for x in coefs]
    return jnp.where(lane4 % 2 == 0, s1, s2), a * c1 + b * c2 + p * s1 + q * s2 + v * z


def in_step(*levels):
    levels = list(levels)
    while levels:
        levels = [level for level in levels if next(level, None) is not None]


def level_step(below, cpad, above, rows_below, rows_above, edge_slope, edge_flux, east, north, land, write, scratch):
    zpad, hpad, gpad, slope, xco, yco, mpad, tops = scratch
    lane = lanes_of((8, LANES))
    first_lane, last_lane = lane == 0, lane == LANES - 1
    mid = slice(8, 72)

    below1, below2 = rows_below(0, 1), rows_below(0, 0)
    above1, above2 = rows_above(0, 0), rows_above(0, 1)
    z_below = rows_below(1, 1) - rows_below(-1, 1)
    z_above = rows_above(1, 0) - rows_above(-1, 0)
    for t in range(NTR):
        zpad[t, mid] = above[t, mid] - below[t, mid]
        cpad[t, 7:8] = below1[t : t + 1]
        cpad[t, 72:73] = above1[t : t + 1]
        tops[0, t : t + 1] = cpad[t, 8:9]
        tops[1, t : t + 1] = cpad[t, 71:72]
    for t in range(2):
        zpad[t, 72:73] = z_above[t : t + 1]
    tops[2] = zpad[0, 8:16]
    tops[3] = zpad[1, 8:16]
    mpad[mid] = land
    mpad[72:73] = above1[7:8]

    yield True

    def at_edge(x, r, f):
        return roll(x, -(32 * (r % 4) + 4 * f + 2 * (r // 4) + 1))

    def x_face(t):
        c, z = cpad[t, mid], zpad[t, mid]
        return roll(c, -1) - c, z + roll(z, -1)

    (dt, zt), (ds, zs) = x_face(0), x_face(1)
    mask = land * roll(land, -1)
    a, b, p, q, v = face_coefficients(east * mask, mask, density(dt, ds), density(zt, zs))
    for i, x in enumerate((a, p, v, roll(b, 1), roll(q, 1), roll(v, 1))):
        xco[i] = x
    yield True

    def y_face(t):
        return cpad[t, 9:73] - cpad[t, mid], zpad[t, mid] + zpad[t, 9:73]

    (dt, zt), (ds, zs) = y_face(0), y_face(1)
    mask = land * mpad[9:73]
    for i, x in enumerate(face_coefficients(north * mask, mask, density(dt, ds), density(zt, zs))):
        yco[i, mid] = x
    row0 = tops[0]
    mask = below1[7:8] * mpad[8:9]
    d = row0 - below1
    a, b, p, q, v = face_coefficients(
        below1[6:7] * mask,
        mask,
        density(d[0:1], d[1:2]),
        density(z_below[0:1] + tops[2, 0:1], z_below[1:2] + tops[3, 0:1]),
    )
    yco[1, 7:8], yco[3, 7:8], yco[4, 7:8] = b, q, v
    h_below = a * below1 + p * minmod(d, below1 - below2) + v * z_below
    b, q, v = yco[1, 71:72], yco[3, 71:72], yco[4, 71:72]
    g_above = b * above1 + q * minmod(above2 - above1, above1 - tops[1]) + v * z_above
    for t in range(NTR):
        hpad[t, 7:8] = h_below[t : t + 1]
        gpad[t, 72:73] = g_above[t : t + 1]

    yield True
    at_side = jnp.logical_or(first_lane, last_lane)
    for r in range(8):
        here = slice(8 + 8 * r, 16 + 8 * r)
        lower, upper = slice(7 + 8 * r, 15 + 8 * r), slice(9 + 8 * r, 17 + 8 * r)
        ya, yp, yv, yb, yq, yw = yco[0, here], yco[2, here], yco[4, here], yco[1, lower], yco[3, lower], yco[4, lower]
        for t in range(NTR):
            c, z = cpad[t, here], zpad[t, here]
            s = minmod(roll(c, -1) - c, c - roll(c, 1))
            slope[t, 8 * r : 8 * r + 8] = jnp.where(at_side, at_edge(edge_slope, r, t), s)
            s = minmod(cpad[t, upper] - c, c - cpad[t, lower])
            hpad[t, here] = ya * c + yp * s + yv * z
            gpad[t, here] = yb * c + yq * s + yw * z
        yield True
    for r in range(8):
        here = slice(8 + 8 * r, 16 + 8 * r)
        lower, upper = slice(7 + 8 * r, 15 + 8 * r), slice(9 + 8 * r, 17 + 8 * r)
        part = slice(8 * r, 8 * r + 8)
        xa, xp, xv, xb, xq, xw = [xco[i, part] for i in range(6)]
        wet = mpad[here]
        for t in range(NTR):
            c, z, s = cpad[t, here], zpad[t, here], slope[t, part]
            h = xa * c + xp * s + xv * z
            g = xb * c + xq * s + xw * z
            flux = at_edge(edge_flux, r, t)
            out_east = jnp.where(last_lane, flux, h + roll(g, -1))
            in_west = jnp.where(first_lane, flux, g + roll(h, 1))
            out_north = hpad[t, here] + gpad[t, upper]
            in_south = hpad[t, lower] + gpad[t, here]
            write(t, part, wet * (c - (out_east - in_west) - (out_north - in_south)))
        yield True


def level_scratch():
    padded = pltpu.VMEM((NTR, 80, LANES), F32)
    return [
        padded,
        padded,
        padded,
        pltpu.VMEM((NTR, ROWS, LANES), F32),
        pltpu.VMEM((6, ROWS, LANES), F32),
        pltpu.VMEM((5, 80, LANES), F32),
        pltpu.VMEM((80, LANES), F32),
        pltpu.VMEM((4, 8, LANES), F32),
    ]


def chunk_spans(lo, hi):
    spans, size = [], 4
    while lo < hi:
        end = min(lo + size, hi)
        if hi - end < size:
            end = hi
        spans.append((lo, end))
        lo, size = end, size + 2
    return spans


def deep_kernel(
    first, together, tracers, east, north, mask, west_cols, east_cols, own_cols, row_below, row_above, out,
    cells, flows_e, flows_n, lands, west_v, east_v, own_v, below_v, above_v, results, edges, halo_sem, level_sem, out_sem, *scratch
):
    levels = cells.shape[1]

    def halo_copies():
        pairs = ((row_below, below_v), (row_above, above_v), (west_cols, west_v), (east_cols, east_v), (own_cols, own_v))
        return [pltpu.make_async_copy(a, b, halo_sem.at[i]) for i, (a, b) in enumerate(pairs)]

    spans = chunk_spans(first - 1, levels)
    sends = chunk_spans(first, levels)[::-1]
    sends = [(first + levels - hi, first + levels - lo) for lo, hi in sends]

    def cell_copy(i):
        lo, hi = spans[i]
        return pltpu.make_async_copy(tracers.at[:, lo:hi], cells.at[:, lo:hi, 8:72], level_sem.at[0, i])

    def flow_copies(i):
        lo, hi = spans[i]
        pairs = ((east, flows_e), (north, flows_n), (mask, lands))
        return [pltpu.make_async_copy(a.at[lo:hi], b.at[lo:hi], level_sem.at[1 + j, i]) for j, (a, b) in enumerate(pairs)]

    def out_copy(i):
        lo, hi = sends[i]
        return pltpu.make_async_copy(results.at[:, lo - first : hi - first], out.at[:, lo:hi], out_sem.at[i])

    cell_copy(0).start()
    for copy in flow_copies(0) + halo_copies():
        copy.start()
    for i in range(1, len(spans)):
        cell_copy(i).start()
        for copy in flow_copies(i):
            copy.start()
    for copy in halo_copies():
        copy.wait()
    for lo in range(first, levels, EDGE_LEVELS):
        ks = range(lo, min(lo + EDGE_LEVELS, levels))
        stacked = (8 * len(ks), LANES)
        lane_of_four = lanes_of(stacked) % 4

        def stack(ref, j, h):
            return jnp.concatenate([ref[min(k + j, levels - 1), h] for k in ks], 0)

        slopes, fluxes = edge_values(
            lambda j, h: jnp.where(lane_of_four < 2, stack(west_v, j, h), stack(east_v, j, h)),
            lambda j, h: stack(own_v, j, h),
        )
        for i, k in enumerate(ks):
            edges[k, 0] = slopes[8 * i : 8 * i + 8]
            edges[k, 1] = fluxes[8 * i : 8 * i + 8]
    for copy in flow_copies(0) + [cell_copy(0)]:
        copy.wait()

    def several(i, _):
        k0 = first + i * together
        for i in range(1, len(spans)):

            @pl.when(jnp.logical_and(k0 + together >= spans[i][0], k0 < spans[i][0]))
            def _():
                for copy in flow_copies(i) + [cell_copy(i)]:
                    copy.wait()

        size = len(scratch) // together
        in_step(*[one(k0 + j, scratch[j * size : (j + 1) * size]) for j in range(together)])
        for i in range(len(sends)):

            @pl.when(k0 + together == sends[i][1])
            def _():
                out_copy(i).start()

        return 0

    def one(k, scratch):
        level = {-1: k - 1, 0: k, 1: jnp.minimum(k + 1, levels - 1)}

        def write(t, part, value):
            results[t, k - first, part] = value

        return level_step(
            cells.at[:, k - 1],
            cells.at[:, k],
            cells.at[:, level[1]],
            lambda j, i: below_v[level[j], i],
            lambda j, i: above_v[level[j], i],
            edges[k, 0],
            edges[k, 1],
            flows_e[k],
            flows_n[k],
            lands[k].astype(F32),
            write,
            scratch,
        )

    lax.fori_loop(0, (levels - first) // together, several, 0)
    for i in range(len(sends)):
        out_copy(i).wait()


def deep_levels(first, tracers, east, north, mask, west_cols, east_cols, own_cols, row_below, row_above):
    levels = tracers.shape[1]
    halos = (west_cols, east_cols, own_cols, row_below, row_above)
    flow = (levels, ROWS, LANES)
    return pl.pallas_call(
        functools.partial(deep_kernel, first, TOGETHER),
        in_specs=[pl.BlockSpec(memory_space=pl.ANY)] * 9,
        out_specs=pl.BlockSpec(memory_space=pl.ANY),
        out_shape=jax.ShapeDtypeStruct(tracers.shape, F32),
        scratch_shapes=[
            pltpu.VMEM((NTR, levels, ROWS + 16, LANES), F32),
            pltpu.VMEM(flow, F32),
            pltpu.VMEM(flow, F32),
            pltpu.VMEM(flow, jnp.int32),
        ]
        + [pltpu.VMEM(x.shape, F32) for x in halos]
        + [
            pltpu.VMEM((NTR, levels - first, ROWS, LANES), F32),
            pltpu.VMEM((levels, 2, 8, LANES), F32),
            pltpu.SemaphoreType.DMA((5,)),
            pltpu.SemaphoreType.DMA((4, levels)),
            pltpu.SemaphoreType.DMA((levels,)),
        ]
        + level_scratch() * TOGETHER,
        compiler_params=pltpu.CompilerParams(vmem_limit_bytes=24 * 1024 * 1024),
        name="deep_levels",
    )(tracers, east, north, mask, *halos)


def expand(x, lane):
    total = x
    for f in range(2, 6):
        total = jnp.where(lane // 4 == f, roll(x, 4 * (f - 1)), total)
    return jnp.where(lane // 4 == 6, roll(x, 16), total)


def pack_rows(tiles, lane):
    packed = []
    for h in range(2):
        total = jnp.zeros((8, LANES), F32)
        for rr in range(4):
            total = jnp.where(lane // 32 == rr, roll(tiles[4 * h + rr], 32 * rr), total)
        packed.append(total)
    return packed


def force_columns(cols, force, lane):
    field = (lane % 32) // 4
    mask = spread(roll(cols, -28), lane % 32)
    tracer_change = mask * (force * jnp.where(field == 0, HEAT_SCALE, FRESH_SCALE * cols))
    return cols + jnp.where(field < 6, tracer_change, jnp.where(field == 6, STRESS_SCALE * force, 0.0))


def force_rows(rows, mask, heat, fresh, tau):
    field = lax.broadcasted_iota(jnp.int32, (8, LANES), 0)
    tracer_change = mask * jnp.where(field == 0, HEAT_SCALE * heat, FRESH_SCALE * fresh * rows)
    return rows + jnp.where(field < 6, tracer_change, jnp.where(field == 6, STRESS_SCALE * tau, 0.0))


def surface_kernel(
    top, arrived, tracers, east, north, mask, west_cols, east_cols, own_cols, row_below, row_above, _, forcing, out,
    cells, cell_sem, rows_b, rows_a, cols_h, cols_o, *scratch
):
    copy = pltpu.make_async_copy(tracers.at[:, 0:3], cells.at[:, :, 8:72], cell_sem)
    copy.start()
    devices = arrived.shape[0] // (4 * GROUPS)
    stride = 4 * GROUPS
    lane = lanes_of((8, LANES))
    lane_of_four = lane % 4

    def gathered(group, row):
        return arrived[pl.ds(4 * group + row, devices, stride=stride), :]

    labels = gathered(4, 0).T
    row_id = lax.broadcasted_iota(jnp.int32, (ROWS, devices), 0).astype(F32) + 1.0

    def pick(n):
        return (labels[n : n + 1] == row_id).astype(F32)

    def dot(a, b):
        return jnp.dot(a, b, precision=lax.Precision.HIGHEST, preferred_element_type=F32)

    flux = jnp.zeros((ROWS, 4 * LANES), F32)
    for n in range(4):
        flux += dot(pick(n), jnp.concatenate([gathered(n, f) for f in range(4)], 1))
    fields = [flux[:, LANES * f : LANES * (f + 1)] for f in range(4)]
    for f in range(4):
        forcing[f] = fields[f]
    heat, fresh, tau_x, tau_y = fields

    wide = lanes_of((devices, LANES))
    sides = [gathered(5, f) for f in range(3)]
    beside = jnp.zeros((ROWS, LANES), F32)
    for side in range(2):
        for n in range(4):
            back = -4 * n - 16 * side
            lined = jnp.where(
                wide < 4, roll(sides[0], back), jnp.where(wide < 8, roll(sides[1], back + 4), roll(sides[2], back + 8))
            )
            lined = jnp.where((wide < 12) & (wide % 4 // 2 == side), lined, 0.0)
            beside += dot(pick(4 + 4 * side + n), lined)

    over = [jnp.sum(gathered(6, f), 0, keepdims=True) for f in range(4)]
    under = [jnp.sum(gathered(7, f), 0, keepdims=True) for f in range(4)]
    tau_under = jnp.sum(gathered(4, 1), 0, keepdims=True)

    land = [mask[k].astype(F32) for k in range(2)]
    copy.wait()
    cells[0, 0, 8:72] = cells[0, 0, 8:72] + land[0] * (HEAT_SCALE * heat)
    for t in range(1, NTR):
        c = cells[t, 0, 8:72]
        cells[t, 0, 8:72] = c + land[0] * (FRESH_SCALE * fresh * c)
    rows_b[0] = force_rows(row_below[0, 0], row_below[0, 0, 7:8], under[2], under[3], 0.0)
    rows_b[1] = force_rows(row_below[0, 1], row_below[0, 1, 7:8], under[0], under[1], tau_under)
    near = jnp.where(top[0] > 0, row_above[0, 1, 7:8], row_above[0, 0, 7:8])
    rows_a[0] = force_rows(row_above[0, 0], near, over[0], over[1], 0.0)
    rows_a[1] = force_rows(row_above[0, 1], row_above[0, 1, 7:8], over[2], over[3], 0.0)
    own_tiles, halo_tiles = [], []
    for r in range(8):
        part = slice(8 * r, 8 * r + 8)
        mine = jnp.where(lane < 4, roll(heat[part], 2), jnp.where(lane < 8, roll(fresh[part], 6), roll(tau_x[part], 10)))
        own_tiles.append(expand(mine, lane))
        halo_tiles.append(expand(beside[part], lane))
    own_force, halo_force = pack_rows(own_tiles, lane), pack_rows(halo_tiles, lane)
    for h in range(2):
        cols = jnp.where(lane_of_four < 2, west_cols[0, h], east_cols[0, h])
        cols_h[h] = force_columns(cols, halo_force[h], lane)
        cols_o[h] = force_columns(own_cols[0, h], own_force[h], lane)

    def level(k):
        def at(j):
            return max(k + j, 0)

        def write(t, part, value):
            out[t, k, part] = value

        size = len(scratch) // 2
        return level_step(
            cells.at[:, at(-1)],
            cells.at[:, k],
            cells.at[:, k + 1],
            lambda j, i: rows_b[i] if at(j) == 0 else row_below[at(j), i],
            lambda j, i: rows_a[i] if at(j) == 0 else row_above[at(j), i],
            slopes[8 * k : 8 * k + 8],
            fluxes[8 * k : 8 * k + 8],
            east[k] + STRESS_SCALE * tau_x if k == 0 else east[k],
            north[k] + STRESS_SCALE * tau_y if k == 0 else north[k],
            land[k],
            write,
            scratch[size * k : size * (k + 1)],
        )

    def halo_at(k, h):
        return cols_h[h] if k <= 0 else jnp.where(lane_of_four < 2, west_cols[k, h], east_cols[k, h])

    def own_at(k, h):
        return cols_o[h] if k <= 0 else own_cols[k, h]

    slopes, fluxes = edge_values(
        lambda j, h: jnp.concatenate([halo_at(k + j, h) for k in range(2)], 0),
        lambda j, h: jnp.concatenate([own_at(k + j, h) for k in range(2)], 0),
    )
    in_step(level(0), level(1))


def surface_levels(top, arrived, tracers, east, north, mask, west_cols, east_cols, own_cols, row_below, row_above, done):
    block = lambda n: pl.BlockSpec((NTR, n, ROWS, LANES), lambda i: (0, 0, 0, 0))
    flow = pl.BlockSpec((2, ROWS, LANES), lambda i: (0, 0, 0))
    halo = lambda x: pl.BlockSpec((3,) + x.shape[1:], lambda i: (0, 0, 0, 0))
    return pl.pallas_call(
        surface_kernel,
        grid=(1,),
        in_specs=[
            pl.BlockSpec(memory_space=pltpu.SMEM),
            pl.BlockSpec(arrived.shape, lambda i: (0, 0)),
            pl.BlockSpec(memory_space=pl.ANY),
            flow,
            flow,
            flow,
        ]
        + [halo(x) for x in (west_cols, east_cols, own_cols, row_below, row_above)]
        + [pl.BlockSpec(memory_space=pl.ANY)],
        out_specs=[pl.BlockSpec((4, ROWS, LANES), lambda i: (0, 0, 0)), block(2)],
        out_shape=[jax.ShapeDtypeStruct((4, ROWS, LANES), F32), jax.ShapeDtypeStruct(tracers.shape, F32)],
        input_output_aliases={11: 1},
        scratch_shapes=[
            pltpu.VMEM((NTR, 3, ROWS + 16, LANES), F32),
            pltpu.SemaphoreType.DMA,
            pltpu.VMEM((2, 8, LANES), F32),
            pltpu.VMEM((2, 8, LANES), F32),
            pltpu.VMEM((2, 8, LANES), F32),
            pltpu.VMEM((2, 8, LANES), F32),
        ]
        + level_scratch() * 2,
        compiler_params=pltpu.CompilerParams(vmem_limit_bytes=VMEM_LIMIT),
        name="surface_levels",
    )(top, arrived, tracers, east, north, mask, west_cols, east_cols, own_cols, row_below, row_above, done)


def fold_ghost(own_top, west_top, c, n_lon, n_lat):
    low = c % LANES
    lane = jnp.arange(LANES)
    joined = jnp.where(lane <= low, own_top, west_top)
    reverse = (lane[:, None] == (low - lane[None, :]) % LANES).astype(F32)
    strip = jnp.einsum("kfl,li->kfi", joined, reverse, precision=lax.Precision.HIGHEST, preferred_element_type=F32)

    def move(b):
        pairs = [(q * n_lat + n_lat - 1, ((b - q) % n_lon) * n_lat + n_lat - 1) for q in range(n_lon)]
        return lambda x: lax.ppermute(x, ("lon", "lat"), pairs)

    return lax.switch(c // LANES, [move(b) for b in range(n_lon)], strip)


def body(tracers, flow_east, flow_north, sea_mask, atm_fields, remap_weights, remap_src, remap_dst, fold_partner):
    n_lon, n_lat = lax.axis_size("lon"), lax.axis_size("lat")
    devices = n_lon * n_lat
    lon, lat = lax.axis_index("lon"), lax.axis_index("lat")
    columns = n_lon * LANES
    c = (fold_partner[0] + lon * LANES) % columns

    both, own_cols, up, down = pack_halos(tracers, flow_east, flow_north, sea_mask)
    right = [(i, (i + 1) % n_lon) for i in range(n_lon)]
    left = [(j, i) for i, j in right]
    north = [(i, i + 1) for i in range(n_lat - 1)]
    south = [(j, i) for i, j in north]
    west_cols = lax.ppermute(both, "lon", right)
    east_cols = lax.ppermute(own_cols, "lon", left)
    row_below = lax.ppermute(up, "lat", north)
    row_above = lax.ppermute(down, "lat", south)
    atm_fields, _ = lax.optimization_barrier((atm_fields, both))
    outgoing = remap(atm_fields, remap_weights, remap_src, remap_dst, c[None], n_lon, n_lat)
    west_cols, outgoing = lax.optimization_barrier((west_cols, outgoing))
    ghost = fold_ghost(both[:, 2], west_cols[:, 2], c, n_lon, n_lat)
    outgoing, ghost, east_cols, row_below, row_above = lax.optimization_barrier(
        (outgoing, ghost, east_cols, row_below, row_above)
    )
    arrived = lax.all_to_all(
        outgoing.reshape(devices, 4 * GROUPS, LANES), ("lon", "lat"), split_axis=0, concat_axis=0, tiled=True
    )
    is_top = lat == n_lat - 1
    field = jnp.arange(8)[:, None]
    ghost_rows = jnp.stack([jnp.where(field == 7, 1.0, ghost), ghost], 1)
    row_above = jnp.where(is_top, ghost_rows, row_above)
    halos = (west_cols, east_cols, own_cols, row_below, row_above)

    done = deep_levels(2, tracers, flow_east, flow_north, sea_mask, *halos)
    top = is_top.astype(jnp.int32)[None]
    return surface_levels(
        top, arrived.reshape(devices * 4 * GROUPS, LANES), tracers, flow_east, flow_north, sea_mask, *halos, done
    )


def solution(mesh):
    placed = (
        P(None, None, "lat", "lon"),
        P(None, "lat", "lon"),
        P(None, "lat", "lon"),
        P(None, "lat", "lon"),
        P(None, ("lon", "lat")),
        P(("lon", "lat"), None, None),
        P(("lon", "lat")),
        P(("lon", "lat")),
        P("lon"),
    )
    return jax.shard_map(
        body,
        mesh=mesh,
        in_specs=placed,
        out_specs=(P(None, "lat", "lon"), P(None, None, "lat", "lon")),
        check_vma=False,
    )
```

```python
import functools

import jax
import jax.numpy as jnp
from jax import lax
from jax.experimental import pallas as pl
from jax.experimental.pallas import tpu as pltpu
from jax.sharding import PartitionSpec as P

HEAT_SCALE = 0.1
FRESH_SCALE = 0.03
STRESS_SCALE = 0.02
HEAT_ALPHA_COEFF = 0.2
SALT_BETA_COEFF = 0.8
SLOPE_EPS = 0.5
DIFFUSIVITY = 0.1

NTR = 6
ROWS = 64
LANES = 128
GROUPS = 7
LABEL_LANE = 32
F32 = jnp.float32
TOGETHER = 2
EDGE_LEVELS = 8
VMEM_LIMIT = 56 * 1024 * 1024


def roll(x, shift):
    return pltpu.roll(x, shift % LANES, axis=1)


def lanes_of(shape):
    return lax.broadcasted_iota(jnp.int32, shape, len(shape) - 1)


def pack_kernel(
    tracers, east, north, mask, both_out, cols_out, up_out, down_out,
    cells, flows_e, flows_n, lands, both_ref, cols_ref, up_ref, down_ref, in_sem, out_sem
):
    lane_group = lanes_of((8, LANES)) // 4
    levels = east.shape[0]
    step = 4
    chunks = levels // step

    def in_copies(i):
        part = pl.ds(i * step, step)
        pairs = ((east, flows_e), (north, flows_n), (mask, lands))
        copies = [pltpu.make_async_copy(a.at[part], b.at[part], in_sem.at[j, i]) for j, (a, b) in enumerate(pairs)]
        return copies + [pltpu.make_async_copy(tracers.at[:, part], cells.at[:, part], in_sem.at[3, i])]

    def out_copies(i):
        part = pl.ds(i * step, step)
        pairs = ((both_ref, both_out), (cols_ref, cols_out), (up_ref, up_out), (down_ref, down_out))
        return [pltpu.make_async_copy(a.at[part], b.at[part], out_sem.at[j, i]) for j, (a, b) in enumerate(pairs)]

    for i in range(chunks):
        for copy in in_copies(i):
            copy.start()

    def chunk(i, _):
        for copy in in_copies(i):
            copy.wait()
        for j in range(step):
            one(i * step + j)
        for copy in out_copies(i):
            copy.start()
        return 0

    def one(k):
        land = lands[k].astype(F32)
        for h in range(2):
            total = jnp.zeros((8, LANES), F32)
            for rr in range(4):
                start = (4 * h + rr) * 8
                for f in range(8):
                    if f < NTR:
                        tile = cells[f, k, start : start + 8]
                    else:
                        tile = land[start : start + 8] if f == 7 else flows_e[k, start : start + 8]
                    moved = roll(tile, 2 + 32 * rr + 4 * f)
                    total = jnp.where(lane_group == 8 * rr + f, moved, total)
            both_ref[k, h] = total
            cols_ref[k, h] = total

        def row(f, r):
            if f < NTR:
                return cells[f, k, r : r + 1]
            return land[r : r + 1] if f == 7 else flows_n[k, r : r + 1]

        for f in range(8):
            last = row(f, ROWS - 1)
            both_ref[k, 2, f : f + 1] = last
            up_ref[k, 0, f : f + 1] = row(f, ROWS - 2)
            up_ref[k, 1, f : f + 1] = last
            for i in range(2):
                down_ref[k, i, f : f + 1] = row(f, i)

    lax.fori_loop(0, chunks, chunk, 0)
    for i in range(chunks):
        for copy in out_copies(i):
            copy.wait()


def pack_halos(tracers, east, north, mask):
    levels = east.shape[0]
    sizes = [(levels, n, 8, LANES) for n in (3, 2, 2, 2)]
    flow = (levels, ROWS, LANES)
    return pl.pallas_call(
        pack_kernel,
        in_specs=[pl.BlockSpec(memory_space=pltpu.HBM)] * 4,
        out_specs=[pl.BlockSpec(memory_space=pl.ANY)] * 4,
        out_shape=[jax.ShapeDtypeStruct(x, F32) for x in sizes],
        scratch_shapes=[
            pltpu.VMEM(tracers.shape, F32),
            pltpu.VMEM(flow, F32),
            pltpu.VMEM(flow, F32),
            pltpu.VMEM(flow, jnp.int32),
        ]
        + [pltpu.VMEM(x, F32) for x in sizes]
        + [pltpu.SemaphoreType.DMA((4, 6)), pltpu.SemaphoreType.DMA((4, 6))],
        compiler_params=pltpu.CompilerParams(vmem_limit_bytes=VMEM_LIMIT),
        name="pack_halos",
    )(tracers, east, north, mask)


def remap_kernel(n_lon, n_lat, src, dst, fold, atm, weights_hbm, out, weights, blocks, edge, labels, count, weight_sem):
    devices = n_lon * n_lat
    sends = weights.shape[0]
    chunks = weight_sem.shape[0]
    per_chunk = sends // chunks

    def weight_copy(i):
        part = pl.ds(i * per_chunk, per_chunk)
        return pltpu.make_async_copy(weights_hbm.at[part], weights.at[part], weight_sem.at[i])

    for i in range(chunks):
        weight_copy(i).start()
    wide = atm[...].astype(F32)
    for b in range(blocks.shape[0]):
        blocks[b, 0:4] = wide[:, b * LANES : (b + 1) * LANES]
    out[...] = jnp.zeros_like(out)
    edge[...] = jnp.zeros_like(edge)
    labels[...] = jnp.zeros_like(labels)

    def clear(i, _):
        count[i] = 0
        return 0

    lax.fori_loop(0, devices, clear, 0, unroll=8)

    lane1 = lanes_of((1, LANES))
    batch = 8

    per = per_chunk // batch

    def chunk(i, _):
        weight_copy(i).wait()
        lax.fori_loop(0, per, lambda j, x: several(i * per + j, x), 0, unroll=per)
        return 0

    def several(i, _):
        places, lefts = [], []
        for j in range(batch):
            w = batch * i + j
            place = dst[w]
            lon = place & (n_lon - 1) if n_lon & (n_lon - 1) == 0 else place % n_lon
            row = place // n_lon
            local = row % ROWS
            owner = lon * n_lat + row // ROWS
            slot = count[owner]
            count[owner] = slot + 1
            kind = jnp.where(local < 2, local, local - (ROWS - 4))
            is_edge = jnp.logical_or(local < 2, local >= ROWS - 2)
            places.append((owner, slot, local, jnp.where(is_edge, owner * 4 + kind, devices * 4)))
            lefts.append(blocks[src[w], 0:4])
        left = jnp.concatenate(lefts, 0).astype(jnp.bfloat16)
        right = weights[pl.ds(pl.multiple_of(batch * i, batch), batch)].reshape(batch * LANES, LANES)
        products = lax.dot_general(left, right, (((1,), (1,)), ((), ())), preferred_element_type=F32)
        for j, (owner, slot, local, at) in enumerate(places):
            product = products[4 * j : 4 * j + 4, LANES * j : LANES * (j + 1)]
            out[owner * GROUPS + slot] = product
            labels[pl.ds(owner, 1)] = jnp.where(lane1 == slot, (local + 1).astype(F32), labels[pl.ds(owner, 1)])
            edge[at] = edge[at] + product
        return 0

    lax.fori_loop(0, chunks, chunk, 0)

    lane4 = lanes_of((4, LANES))
    high = fold[0] // LANES
    low = fold[0] % LANES
    strips = []
    for p in range(n_lon):
        first = edge[(((high - p + 2 * n_lon) % n_lon) * n_lat + n_lat - 1) * 4 + 3]
        second = edge[(((high - p - 1 + 2 * n_lon) % n_lon) * n_lat + n_lat - 1) * 4 + 3]
        strips.append(jnp.where(lane4 <= low, first, second))
    ghost = reversed_lanes(jnp.concatenate(strips, 0), low)
    for owner in range(devices):
        total = jnp.zeros((4, LANES), F32)
        for n in range(4):
            moved = roll(out[owner * GROUPS + n], 2 + 4 * n)
            total = jnp.where(lane4 // 4 == n, moved, total)
        out[owner * GROUPS + 4] = total
    own = labels[...]
    lane = lanes_of(own.shape) - LABEL_LANE
    west = jnp.concatenate([own[devices - n_lat :], own[: devices - n_lat]], 0)
    east = jnp.concatenate([own[n_lat:], own[:n_lat]], 0)
    labels[...] = jnp.where(
        lane < 4, roll(own, LABEL_LANE), jnp.where(lane < 8, roll(west, LABEL_LANE + 4), roll(east, LABEL_LANE + 8))
    )
    for lat in range(n_lat):
        packs = [out[(lon * n_lat + lat) * GROUPS + 4] for lon in range(n_lon)]
        for lon in range(n_lon):
            owner = lon * n_lat + lat
            base = owner * GROUPS
            beside = jnp.where(lane4 < 16, packs[(lon - 1) % n_lon], roll(packs[(lon + 1) % n_lon], 16))
            out[base + 4, 0:3] = beside[0:3]
            out[base + 4, 0:1] = beside[0:1] + labels[owner : owner + 1]
            if lat < n_lat - 1:
                above = (owner + 1) * 4
                out[base + 5, 0:2] = edge[above, 0:2]
                out[base + 5, 2:4] = edge[above + 1, 0:2]
            else:
                out[base + 5, 0:2] = ghost[4 * lon : 4 * lon + 2]
                out[base + 5, 2:4] = ghost[4 * lon : 4 * lon + 2]
            if lat > 0:
                below = (owner - 1) * 4
                out[base + 6, 0:2] = edge[below + 3, 0:2]
                out[base + 6, 2:4] = edge[below + 2, 0:2]
                out[base + 4, 3:4] = edge[below + 3, 3:4]
            else:
                out[base + 4, 3:4] = jnp.zeros((1, LANES), F32)


def reversed_lanes(x, low):
    before = lax.broadcasted_iota(jnp.int32, (LANES, LANES), 0)
    after = lax.broadcasted_iota(jnp.int32, (LANES, LANES), 1)
    table = (before == (low - after + LANES) % LANES).astype(F32)
    return jnp.dot(x, table, precision=lax.Precision.HIGHEST, preferred_element_type=F32)


def remap(atm, weights, src, dst, fold_c, n_lon, n_lat):
    devices = n_lon * n_lat
    blocks = atm.shape[1] // LANES
    smem = pl.BlockSpec(memory_space=pltpu.SMEM)
    return pl.pallas_call(
        functools.partial(remap_kernel, n_lon, n_lat),
        in_specs=[smem, smem, smem, pl.BlockSpec(memory_space=pltpu.VMEM), pl.BlockSpec(memory_space=pltpu.HBM)],
        out_specs=pl.BlockSpec(memory_space=pltpu.VMEM),
        out_shape=jax.ShapeDtypeStruct((devices * GROUPS, 4, LANES), F32),
        scratch_shapes=[
            pltpu.VMEM(weights.shape, weights.dtype),
            pltpu.VMEM((blocks, 8, LANES), F32),
            pltpu.VMEM((devices * 4 + 1, 4, LANES), F32),
            pltpu.VMEM((devices, LANES), F32),
            pltpu.SMEM((devices,), jnp.int32),
            pltpu.SemaphoreType.DMA((8,)),
        ],
        compiler_params=pltpu.CompilerParams(vmem_limit_bytes=VMEM_LIMIT),
        name="remap",
    )(src, dst, fold_c, atm, weights)


def minmod(a, b):
    return jnp.maximum(jnp.minimum(a, b), jnp.minimum(jnp.maximum(a, b), 0.0))


def face_coefficients(flow, mask, drho, zrho):
    diff = DIFFUSIVITY * mask
    strat = 0.25 * zrho
    slope = drho * strat / (strat * strat + SLOPE_EPS)
    up = jnp.maximum(flow, 0.0)
    down = jnp.minimum(flow, 0.0)
    return (
        up + diff,
        down - diff,
        0.5 * up * (1.0 - up),
        -0.5 * down * (1.0 + down),
        0.25 * diff * slope,
    )


def density(temperature, salinity):
    return SALT_BETA_COEFF * salinity - HEAT_ALPHA_COEFF * temperature


def spread(x, lane32):
    for width in (4, 8, 16):
        x = jnp.where(lane32 < width, x, roll(x, width))
    return x


def edge_values(halo, own):
    lane = lanes_of(halo(0, 0).shape)
    lane4, lane32 = lane % 4, lane % 32
    east = lane4 == 0
    parts = []
    for h in range(2):
        p, o = halo(0, h), own(0, h)
        zp, zo = halo(1, h) - halo(-1, h), own(1, h) - own(-1, h)
        o1, p2, zp2 = roll(o, -1), roll(p, -2), roll(zp, -2)
        zo1 = roll(zo, -1)
        parts.append(
            (
                jnp.where(east, o, roll(p, 1)),
                jnp.where(east, o1, p),
                jnp.where(east, p2, o1),
                jnp.where(east, roll(p, -3), roll(o, -2)),
                jnp.where(east, zo1, zp),
                jnp.where(east, zp2, zo1),
            )
        )
    c0, c1, c2, c3, z1, z2 = [jnp.where(lane4 < 2, x, roll(y, 2)) for x, y in zip(*parts)]
    d2 = c2 - c1
    s1, s2 = minmod(d2, c1 - c0), minmod(c3 - c2, d2)
    z = z1 + z2
    mask = roll(c1 * c2, -28)
    coefs = face_coefficients(roll(c1, -24) * mask, mask, density(d2, roll(d2, -4)), density(z, roll(z, -4)))
    a, b, p, q, v = [spread(x, lane32) for x in coefs]
    return jnp.where(lane4 % 2 == 0, s1, s2), a * c1 + b * c2 + p * s1 + q * s2 + v * z


def in_step(*levels):
    levels = list(levels)
    while levels:
        levels = [level for level in levels if next(level, None) is not None]


def level_step(below, cpad, above, rows_below, rows_above, edge_slope, edge_flux, east, north, land, write, scratch):
    zpad, hpad, gpad, slope, xco, yco, mpad, tops = scratch
    lane = lanes_of((8, LANES))
    first_lane, last_lane = lane == 0, lane == LANES - 1
    mid = slice(8, 72)

    below1, below2 = rows_below(0, 1), rows_below(0, 0)
    above1, above2 = rows_above(0, 0), rows_above(0, 1)
    z_below = rows_below(1, 1) - rows_below(-1, 1)
    z_above = rows_above(1, 0) - rows_above(-1, 0)
    for t in range(NTR):
        zpad[t, mid] = above[t, mid] - below[t, mid]
        cpad[t, 7:8] = below1[t : t + 1]
        cpad[t, 72:73] = above1[t : t + 1]
        tops[0, t : t + 1] = cpad[t, 8:9]
        tops[1, t : t + 1] = cpad[t, 71:72]
    for t in range(2):
        zpad[t, 72:73] = z_above[t : t + 1]
    tops[2] = zpad[0, 8:16]
    tops[3] = zpad[1, 8:16]
    mpad[mid] = land
    mpad[72:73] = above1[7:8]

    yield True

    def at_edge(x, r, f):
        return roll(x, -(32 * (r % 4) + 4 * f + 2 * (r // 4) + 1))

    def x_face(t):
        c, z = cpad[t, mid], zpad[t, mid]
        return roll(c, -1) - c, z + roll(z, -1)

    (dt, zt), (ds, zs) = x_face(0), x_face(1)
    mask = land * roll(land, -1)
    a, b, p, q, v = face_coefficients(east * mask, mask, density(dt, ds), density(zt, zs))
    for i, x in enumerate((a, p, v, roll(b, 1), roll(q, 1), roll(v, 1))):
        xco[i] = x
    yield True

    def y_face(t):
        return cpad[t, 9:73] - cpad[t, mid], zpad[t, mid] + zpad[t, 9:73]

    (dt, zt), (ds, zs) = y_face(0), y_face(1)
    mask = land * mpad[9:73]
    for i, x in enumerate(face_coefficients(north * mask, mask, density(dt, ds), density(zt, zs))):
        yco[i, mid] = x
    row0 = tops[0]
    mask = below1[7:8] * mpad[8:9]
    d = row0 - below1
    a, b, p, q, v = face_coefficients(
        below1[6:7] * mask,
        mask,
        density(d[0:1], d[1:2]),
        density(z_below[0:1] + tops[2, 0:1], z_below[1:2] + tops[3, 0:1]),
    )
    yco[1, 7:8], yco[3, 7:8], yco[4, 7:8] = b, q, v
    h_below = a * below1 + p * minmod(d, below1 - below2) + v * z_below
    b, q, v = yco[1, 71:72], yco[3, 71:72], yco[4, 71:72]
    g_above = b * above1 + q * minmod(above2 - above1, above1 - tops[1]) + v * z_above
    for t in range(NTR):
        hpad[t, 7:8] = h_below[t : t + 1]
        gpad[t, 72:73] = g_above[t : t + 1]

    yield True
    at_side = jnp.logical_or(first_lane, last_lane)
    for r in range(8):
        here = slice(8 + 8 * r, 16 + 8 * r)
        lower, upper = slice(7 + 8 * r, 15 + 8 * r), slice(9 + 8 * r, 17 + 8 * r)
        ya, yp, yv, yb, yq, yw = yco[0, here], yco[2, here], yco[4, here], yco[1, lower], yco[3, lower], yco[4, lower]
        for t in range(NTR):
            c, z = cpad[t, here], zpad[t, here]
            s = minmod(roll(c, -1) - c, c - roll(c, 1))
            slope[t, 8 * r : 8 * r + 8] = jnp.where(at_side, at_edge(edge_slope, r, t), s)
            s = minmod(cpad[t, upper] - c, c - cpad[t, lower])
            hpad[t, here] = ya * c + yp * s + yv * z
            gpad[t, here] = yb * c + yq * s + yw * z
        yield True
    for r in range(8):
        here = slice(8 + 8 * r, 16 + 8 * r)
        lower, upper = slice(7 + 8 * r, 15 + 8 * r), slice(9 + 8 * r, 17 + 8 * r)
        part = slice(8 * r, 8 * r + 8)
        xa, xp, xv, xb, xq, xw = [xco[i, part] for i in range(6)]
        wet = mpad[here]
        for t in range(NTR):
            c, z, s = cpad[t, here], zpad[t, here], slope[t, part]
            h = xa * c + xp * s + xv * z
            g = xb * c + xq * s + xw * z
            flux = at_edge(edge_flux, r, t)
            out_east = jnp.where(last_lane, flux, h + roll(g, -1))
            in_west = jnp.where(first_lane, flux, g + roll(h, 1))
            out_north = hpad[t, here] + gpad[t, upper]
            in_south = hpad[t, lower] + gpad[t, here]
            write(t, part, wet * (c - (out_east - in_west) - (out_north - in_south)))
        yield True


def level_scratch():
    padded = pltpu.VMEM((NTR, 80, LANES), F32)
    return [
        padded,
        padded,
        padded,
        pltpu.VMEM((NTR, ROWS, LANES), F32),
        pltpu.VMEM((6, ROWS, LANES), F32),
        pltpu.VMEM((5, 80, LANES), F32),
        pltpu.VMEM((80, LANES), F32),
        pltpu.VMEM((4, 8, LANES), F32),
    ]


def chunk_spans(lo, hi):
    spans, size = [], 4
    while lo < hi:
        end = min(lo + size, hi)
        if hi - end < size:
            end = hi
        spans.append((lo, end))
        lo, size = end, size + 2
    return spans


def deep_kernel(
    first, together, top, tracers, east, north, mask, west_cols, east_cols, own_cols, row_below, row_above, ghost, out,
    cells, flows_e, flows_n, lands, west_v, east_v, own_v, below_v, above_v, ghost_v, results, edges, halo_sem, level_sem, out_sem, *scratch
):
    levels = cells.shape[1]

    def halo_copies():
        pairs = ((row_below, below_v), (row_above, above_v), (west_cols, west_v), (east_cols, east_v), (own_cols, own_v), (ghost, ghost_v))
        return [pltpu.make_async_copy(a, b, halo_sem.at[i]) for i, (a, b) in enumerate(pairs)]

    spans = chunk_spans(first - 1, levels)
    sends = chunk_spans(first, levels)[::-1]
    sends = [(first + levels - hi, first + levels - lo) for lo, hi in sends]

    def cell_copy(i):
        lo, hi = spans[i]
        return pltpu.make_async_copy(tracers.at[:, lo:hi], cells.at[:, lo:hi, 8:72], level_sem.at[0, i])

    def flow_copies(i):
        lo, hi = spans[i]
        pairs = ((east, flows_e), (north, flows_n), (mask, lands))
        return [pltpu.make_async_copy(a.at[lo:hi], b.at[lo:hi], level_sem.at[1 + j, i]) for j, (a, b) in enumerate(pairs)]

    def out_copy(i):
        lo, hi = sends[i]
        return pltpu.make_async_copy(results.at[:, lo - first : hi - first], out.at[:, lo:hi], out_sem.at[i])

    cell_copy(0).start()
    for copy in flow_copies(0) + halo_copies():
        copy.start()
    for i in range(1, len(spans)):
        cell_copy(i).start()
        for copy in flow_copies(i):
            copy.start()
    for copy in halo_copies():
        copy.wait()

    @pl.when(top[0] > 0)
    def _():
        field = lax.broadcasted_iota(jnp.int32, ghost_v.shape, 1)
        above_v[:, 0] = jnp.where(field == 7, 1.0, ghost_v[...])
        above_v[:, 1] = ghost_v[...]

    for lo in range(first, levels, EDGE_LEVELS):
        ks = range(lo, min(lo + EDGE_LEVELS, levels))
        stacked = (8 * len(ks), LANES)
        lane_of_four = lanes_of(stacked) % 4

        def stack(ref, j, h):
            return jnp.concatenate([ref[min(k + j, levels - 1), h] for k in ks], 0)

        slopes, fluxes = edge_values(
            lambda j, h: jnp.where(lane_of_four < 2, stack(west_v, j, h), stack(east_v, j, h)),
            lambda j, h: stack(own_v, j, h),
        )
        for i, k in enumerate(ks):
            edges[k, 0] = slopes[8 * i : 8 * i + 8]
            edges[k, 1] = fluxes[8 * i : 8 * i + 8]
    for copy in flow_copies(0) + [cell_copy(0)]:
        copy.wait()

    def several(i, _):
        k0 = first + i * together
        for i in range(1, len(spans)):

            @pl.when(jnp.logical_and(k0 + together >= spans[i][0], k0 < spans[i][0]))
            def _():
                for copy in flow_copies(i) + [cell_copy(i)]:
                    copy.wait()

        size = len(scratch) // together
        in_step(*[one(k0 + j, scratch[j * size : (j + 1) * size]) for j in range(together)])
        for i in range(len(sends)):

            @pl.when(k0 + together == sends[i][1])
            def _():
                out_copy(i).start()

        return 0

    def one(k, scratch):
        level = {-1: k - 1, 0: k, 1: jnp.minimum(k + 1, levels - 1)}

        def write(t, part, value):
            results[t, k - first, part] = value

        return level_step(
            cells.at[:, k - 1],
            cells.at[:, k],
            cells.at[:, level[1]],
            lambda j, i: below_v[level[j], i],
            lambda j, i: above_v[level[j], i],
            edges[k, 0],
            edges[k, 1],
            flows_e[k],
            flows_n[k],
            lands[k].astype(F32),
            write,
            scratch,
        )

    lax.fori_loop(0, (levels - first) // together, several, 0)
    for i in range(len(sends)):
        out_copy(i).wait()


def deep_levels(first, top, tracers, east, north, mask, west_cols, east_cols, own_cols, row_below, row_above, ghost):
    levels = tracers.shape[1]
    halos = (west_cols, east_cols, own_cols, row_below, row_above, ghost)
    flow = (levels, ROWS, LANES)
    return pl.pallas_call(
        functools.partial(deep_kernel, first, TOGETHER),
        in_specs=[pl.BlockSpec(memory_space=pltpu.SMEM)]
        + [pl.BlockSpec(memory_space=pltpu.HBM)] * 4
        + [pl.BlockSpec(memory_space=pl.ANY)] * 6,
        out_specs=pl.BlockSpec(memory_space=pl.ANY),
        out_shape=jax.ShapeDtypeStruct(tracers.shape, F32),
        scratch_shapes=[
            pltpu.VMEM((NTR, levels, ROWS + 16, LANES), F32),
            pltpu.VMEM(flow, F32),
            pltpu.VMEM(flow, F32),
            pltpu.VMEM(flow, jnp.int32),
        ]
        + [pltpu.VMEM(x.shape, F32) for x in halos]
        + [
            pltpu.VMEM((NTR, levels - first, ROWS, LANES), F32),
            pltpu.VMEM((levels, 2, 8, LANES), F32),
            pltpu.SemaphoreType.DMA((6,)),
            pltpu.SemaphoreType.DMA((4, levels)),
            pltpu.SemaphoreType.DMA((levels,)),
        ]
        + level_scratch() * TOGETHER,
        compiler_params=pltpu.CompilerParams(vmem_limit_bytes=24 * 1024 * 1024),
        name="deep_levels",
    )(top, tracers, east, north, mask, *halos)


def expand(x, lane):
    total = x
    for f in range(2, 6):
        total = jnp.where(lane // 4 == f, roll(x, 4 * (f - 1)), total)
    return jnp.where(lane // 4 == 6, roll(x, 16), total)


def pack_rows(tiles, lane):
    packed = []
    for h in range(2):
        total = jnp.zeros((8, LANES), F32)
        for rr in range(4):
            total = jnp.where(lane // 32 == rr, roll(tiles[4 * h + rr], 32 * rr), total)
        packed.append(total)
    return packed


def force_columns(cols, force, lane):
    field = (lane % 32) // 4
    mask = spread(roll(cols, -28), lane % 32)
    tracer_change = mask * (force * jnp.where(field == 0, HEAT_SCALE, FRESH_SCALE * cols))
    return cols + jnp.where(field < 6, tracer_change, jnp.where(field == 6, STRESS_SCALE * force, 0.0))


def force_rows(rows, mask, heat, fresh, tau):
    field = lax.broadcasted_iota(jnp.int32, (8, LANES), 0)
    tracer_change = mask * jnp.where(field == 0, HEAT_SCALE * heat, FRESH_SCALE * fresh * rows)
    return rows + jnp.where(field < 6, tracer_change, jnp.where(field == 6, STRESS_SCALE * tau, 0.0))


def surface_kernel(
    top, arrived, tracers, east, north, mask, west_cols, east_cols, own_cols, row_below, arriving_above, ghost, _, forcing, out,
    row_above, cells, cell_sem, rows_b, rows_a, cols_h, cols_o, *scratch
):
    copy = pltpu.make_async_copy(tracers.at[:, 0:3], cells.at[:, :, 8:72], cell_sem)
    copy.start()
    devices = arrived.shape[0] // (4 * GROUPS)
    stride = 4 * GROUPS
    lane = lanes_of((8, LANES))
    lane_of_four = lane % 4

    def gathered(group, row):
        return arrived[pl.ds(4 * group + row, devices, stride=stride), :]

    labels = gathered(4, 0).T[LABEL_LANE : LABEL_LANE + 16]
    row_id = lax.broadcasted_iota(jnp.int32, (ROWS, devices), 0).astype(F32) + 1.0

    def pick(n):
        return (labels[n : n + 1] == row_id).astype(F32)

    def dot(a, b):
        return jnp.dot(a, b, precision=lax.Precision.HIGHEST, preferred_element_type=F32)

    flux = jnp.zeros((ROWS, 4 * LANES), F32)
    for n in range(4):
        flux += dot(pick(n), jnp.concatenate([gathered(n, f) for f in range(4)], 1))
    fields = [flux[:, LANES * f : LANES * (f + 1)] for f in range(4)]
    for f in range(4):
        forcing[f] = fields[f]
    heat, fresh, tau_x, tau_y = fields

    wide = lanes_of((devices, LANES))
    sides = [gathered(4, f) for f in range(3)]
    beside = jnp.zeros((ROWS, LANES), F32)
    for side in range(2):
        for n in range(4):
            back = -4 * n - 16 * side
            lined = jnp.where(
                wide < 4, roll(sides[0], back), jnp.where(wide < 8, roll(sides[1], back + 4), roll(sides[2], back + 8))
            )
            lined = jnp.where((wide < 12) & (wide % 4 // 2 == side), lined, 0.0)
            beside += dot(pick(4 + 4 * side + n), lined)

    over = [jnp.sum(gathered(5, f), 0, keepdims=True) for f in range(4)]
    under = [jnp.sum(gathered(6, f), 0, keepdims=True) for f in range(4)]
    tau_under = jnp.sum(gathered(4, 3), 0, keepdims=True)
    is_top = top[0] > 0
    field = lax.broadcasted_iota(jnp.int32, (8, LANES), 0)
    for k in range(3):
        row_above[k, 0] = jnp.where(is_top, jnp.where(field == 7, 1.0, ghost[k]), arriving_above[k, 0])
        row_above[k, 1] = jnp.where(is_top, ghost[k], arriving_above[k, 1])

    land = [mask[k].astype(F32) for k in range(2)]
    copy.wait()
    cells[0, 0, 8:72] = cells[0, 0, 8:72] + land[0] * (HEAT_SCALE * heat)
    for t in range(1, NTR):
        c = cells[t, 0, 8:72]
        cells[t, 0, 8:72] = c + land[0] * (FRESH_SCALE * fresh * c)
    rows_b[0] = force_rows(row_below[0, 0], row_below[0, 0, 7:8], under[2], under[3], 0.0)
    rows_b[1] = force_rows(row_below[0, 1], row_below[0, 1, 7:8], under[0], under[1], tau_under)
    near = jnp.where(is_top, row_above[0, 1, 7:8], row_above[0, 0, 7:8])
    rows_a[0] = force_rows(row_above[0, 0], near, over[0], over[1], 0.0)
    rows_a[1] = force_rows(row_above[0, 1], row_above[0, 1, 7:8], over[2], over[3], 0.0)
    own_tiles, halo_tiles = [], []
    for r in range(8):
        part = slice(8 * r, 8 * r + 8)
        mine = jnp.where(lane < 4, roll(heat[part], 2), jnp.where(lane < 8, roll(fresh[part], 6), roll(tau_x[part], 10)))
        own_tiles.append(expand(mine, lane))
        halo_tiles.append(expand(beside[part], lane))
    own_force, halo_force = pack_rows(own_tiles, lane), pack_rows(halo_tiles, lane)
    for h in range(2):
        cols = jnp.where(lane_of_four < 2, west_cols[0, h], east_cols[0, h])
        cols_h[h] = force_columns(cols, halo_force[h], lane)
        cols_o[h] = force_columns(own_cols[0, h], own_force[h], lane)

    def level(k):
        def at(j):
            return max(k + j, 0)

        def write(t, part, value):
            out[t, k, part] = value

        size = len(scratch) // 2
        return level_step(
            cells.at[:, at(-1)],
            cells.at[:, k],
            cells.at[:, k + 1],
            lambda j, i: rows_b[i] if at(j) == 0 else row_below[at(j), i],
            lambda j, i: rows_a[i] if at(j) == 0 else row_above[at(j), i],
            slopes[8 * k : 8 * k + 8],
            fluxes[8 * k : 8 * k + 8],
            east[k] + STRESS_SCALE * tau_x if k == 0 else east[k],
            north[k] + STRESS_SCALE * tau_y if k == 0 else north[k],
            land[k],
            write,
            scratch[size * k : size * (k + 1)],
        )

    def halo_at(k, h):
        return cols_h[h] if k <= 0 else jnp.where(lane_of_four < 2, west_cols[k, h], east_cols[k, h])

    def own_at(k, h):
        return cols_o[h] if k <= 0 else own_cols[k, h]

    slopes, fluxes = edge_values(
        lambda j, h: jnp.concatenate([halo_at(k + j, h) for k in range(2)], 0),
        lambda j, h: jnp.concatenate([own_at(k + j, h) for k in range(2)], 0),
    )
    in_step(level(0), level(1))


def surface_levels(top, arrived, tracers, east, north, mask, west_cols, east_cols, own_cols, row_below, row_above, ghost, done):
    block = lambda n: pl.BlockSpec((NTR, n, ROWS, LANES), lambda i: (0, 0, 0, 0))
    flow = pl.BlockSpec((2, ROWS, LANES), lambda i: (0, 0, 0))
    halo = lambda x: pl.BlockSpec((3,) + x.shape[1:], lambda i: (0,) * x.ndim)
    return pl.pallas_call(
        surface_kernel,
        grid=(1,),
        in_specs=[
            pl.BlockSpec(memory_space=pltpu.SMEM),
            pl.BlockSpec(arrived.shape, lambda i: (0, 0)),
            pl.BlockSpec(memory_space=pltpu.HBM),
            flow,
            flow,
            flow,
        ]
        + [halo(x) for x in (west_cols, east_cols, own_cols, row_below, row_above, ghost)]
        + [pl.BlockSpec(memory_space=pltpu.HBM)],
        out_specs=[pl.BlockSpec((4, ROWS, LANES), lambda i: (0, 0, 0)), block(2)],
        out_shape=[jax.ShapeDtypeStruct((4, ROWS, LANES), F32), jax.ShapeDtypeStruct(tracers.shape, F32)],
        input_output_aliases={12: 1},
        scratch_shapes=[
            pltpu.VMEM((3, 2, 8, LANES), F32),
            pltpu.VMEM((NTR, 3, ROWS + 16, LANES), F32),
            pltpu.SemaphoreType.DMA,
            pltpu.VMEM((2, 8, LANES), F32),
            pltpu.VMEM((2, 8, LANES), F32),
            pltpu.VMEM((2, 8, LANES), F32),
            pltpu.VMEM((2, 8, LANES), F32),
        ]
        + level_scratch() * 2,
        compiler_params=pltpu.CompilerParams(vmem_limit_bytes=VMEM_LIMIT),
        name="surface_levels",
    )(top, arrived, tracers, east, north, mask, west_cols, east_cols, own_cols, row_below, row_above, ghost, done)


def strip_kernel(c, own, west, out):
    low = c[0] % LANES
    levels = own.shape[0]
    lane = lanes_of((levels, 8, LANES))
    joined = jnp.where(lane <= low, own[:, 0], west[:, 0]).reshape(levels * 8, LANES)
    out[...] = reversed_lanes(joined, low).reshape(levels, 8, LANES)


def fold_strip(both, west_cols, c):
    levels = both.shape[0]
    top = pl.BlockSpec((levels, 1, 8, LANES), lambda i: (0, 2, 0, 0))
    return pl.pallas_call(
        strip_kernel,
        grid=(1,),
        in_specs=[pl.BlockSpec(memory_space=pltpu.SMEM), top, top],
        out_specs=pl.BlockSpec((levels, 8, LANES), lambda i: (0, 0, 0)),
        out_shape=jax.ShapeDtypeStruct((levels, 8, LANES), F32),
        name="fold_strip",
    )(c, both, west_cols)


def body(tracers, flow_east, flow_north, sea_mask, atm_fields, remap_weights, remap_src, remap_dst, fold_partner):
    n_lon, n_lat = lax.axis_size("lon"), lax.axis_size("lat")
    devices = n_lon * n_lat
    lon, lat = lax.axis_index("lon"), lax.axis_index("lat")
    c = (fold_partner[0] + lon * LANES) % (n_lon * LANES)
    top = (lat == n_lat - 1).astype(jnp.int32)[None]

    both, own_cols, up, down = pack_halos(tracers, flow_east, flow_north, sea_mask)
    right = [(i, (i + 1) % n_lon) for i in range(n_lon)]
    left = [(j, i) for i, j in right]
    north = [(i, i + 1) for i in range(n_lat - 1)]
    south = [(j, i) for i, j in north]
    west_cols = lax.ppermute(both, "lon", right)
    row_below = lax.ppermute(up, "lat", north)
    row_above = lax.ppermute(down, "lat", south)
    east_cols = lax.ppermute(own_cols, "lon", left)
    strip = fold_strip(both, west_cols, c[None])

    def move(b):
        pairs = [(q * n_lat + n_lat - 1, ((b - q) % n_lon) * n_lat + n_lat - 1) for q in range(n_lon)]

        def branch(strip, *operands):
            return lax.ppermute(strip, ("lon", "lat"), pairs), remap(*operands, n_lon, n_lat)

        return branch

    ghost, outgoing = lax.switch(
        c // LANES,
        [move(b) for b in range(n_lon)],
        strip,
        atm_fields,
        remap_weights,
        remap_src,
        remap_dst,
        c[None],
    )
    outgoing, ghost, east_cols, row_below, row_above = lax.optimization_barrier(
        (outgoing, ghost, east_cols, row_below, row_above)
    )
    arrived = lax.all_to_all(outgoing, ("lon", "lat"), split_axis=0, concat_axis=0, tiled=True)
    halos = (west_cols, east_cols, own_cols, row_below, row_above, ghost)
    done = deep_levels(2, top, tracers, flow_east, flow_north, sea_mask, *halos)
    arrived = arrived.reshape(devices * 4 * GROUPS, LANES)
    return surface_levels(top, arrived, tracers, flow_east, flow_north, sea_mask, *halos, done)


def solution(mesh):
    placed = (
        P(None, None, "lat", "lon"),
        P(None, "lat", "lon"),
        P(None, "lat", "lon"),
        P(None, "lat", "lon"),
        P(None, ("lon", "lat")),
        P(("lon", "lat"), None, None),
        P(("lon", "lat")),
        P(("lon", "lat")),
        P("lon"),
    )
    return jax.shard_map(
        body,
        mesh=mesh,
        in_specs=placed,
        out_specs=(P(None, "lat", "lon"), P(None, None, "lat", "lon")),
        check_vma=False,
    )
```

```python
import functools

import jax
import jax.numpy as jnp
from jax import lax
from jax.experimental import pallas as pl
from jax.experimental.pallas import tpu as pltpu
from jax.sharding import PartitionSpec as P

HEAT_SCALE = 0.1
FRESH_SCALE = 0.03
STRESS_SCALE = 0.02
HEAT_ALPHA_COEFF = 0.2
SALT_BETA_COEFF = 0.8
SLOPE_EPS = 0.5
DIFFUSIVITY = 0.1

NTR = 6
ROWS = 64
LANES = 128
GROUPS = 7
LABEL_LANE = 32
F32 = jnp.float32
TOGETHER = 2
EDGE_LEVELS = 8
VMEM_LIMIT = 56 * 1024 * 1024


def roll(x, shift):
    return pltpu.roll(x, shift % LANES, axis=1)


def lanes_of(shape):
    return lax.broadcasted_iota(jnp.int32, shape, len(shape) - 1)


def pack_kernel(
    tracers, east, north, mask, both_out, cols_out, up_out, down_out,
    cells, flows_e, flows_n, lands, both_ref, cols_ref, up_ref, down_ref, in_sem, out_sem
):
    lane_group = lanes_of((8, LANES)) // 4
    levels = east.shape[0]
    step = 4
    chunks = levels // step

    def in_copies(i):
        part = pl.ds(i * step, step)
        pairs = ((east, flows_e), (north, flows_n), (mask, lands))
        copies = [pltpu.make_async_copy(a.at[part], b.at[part], in_sem.at[j, i]) for j, (a, b) in enumerate(pairs)]
        return copies + [pltpu.make_async_copy(tracers.at[:, part], cells.at[:, part], in_sem.at[3, i])]

    def out_copies(i):
        part = pl.ds(i * step, step)
        pairs = ((both_ref, both_out), (cols_ref, cols_out), (up_ref, up_out), (down_ref, down_out))
        return [pltpu.make_async_copy(a.at[part], b.at[part], out_sem.at[j, i]) for j, (a, b) in enumerate(pairs)]

    for i in range(chunks):
        for copy in in_copies(i):
            copy.start()

    def chunk(i, _):
        for copy in in_copies(i):
            copy.wait()
        for j in range(step):
            one(i * step + j)
        for copy in out_copies(i):
            copy.start()
        return 0

    def one(k):
        land = lands[k].astype(F32)
        for h in range(2):
            total = jnp.zeros((8, LANES), F32)
            for rr in range(4):
                start = (4 * h + rr) * 8
                for f in range(8):
                    if f < NTR:
                        tile = cells[f, k, start : start + 8]
                    else:
                        tile = land[start : start + 8] if f == 7 else flows_e[k, start : start + 8]
                    moved = roll(tile, 2 + 32 * rr + 4 * f)
                    total = jnp.where(lane_group == 8 * rr + f, moved, total)
            both_ref[k, h] = total
            cols_ref[k, h] = total

        def row(f, r):
            if f < NTR:
                return cells[f, k, r : r + 1]
            return land[r : r + 1] if f == 7 else flows_n[k, r : r + 1]

        for f in range(8):
            last = row(f, ROWS - 1)
            both_ref[k, 2, f : f + 1] = last
            up_ref[k, 0, f : f + 1] = row(f, ROWS - 2)
            up_ref[k, 1, f : f + 1] = last
            for i in range(2):
                down_ref[k, i, f : f + 1] = row(f, i)

    lax.fori_loop(0, chunks, chunk, 0)
    for i in range(chunks):
        for copy in out_copies(i):
            copy.wait()


def pack_halos(tracers, east, north, mask):
    levels = east.shape[0]
    sizes = [(levels, n, 8, LANES) for n in (3, 2, 2, 2)]
    flow = (levels, ROWS, LANES)
    return pl.pallas_call(
        pack_kernel,
        in_specs=[pl.BlockSpec(memory_space=pltpu.HBM)] * 4,
        out_specs=[pl.BlockSpec(memory_space=pl.ANY)] * 4,
        out_shape=[jax.ShapeDtypeStruct(x, F32) for x in sizes],
        scratch_shapes=[
            pltpu.VMEM(tracers.shape, F32),
            pltpu.VMEM(flow, F32),
            pltpu.VMEM(flow, F32),
            pltpu.VMEM(flow, jnp.int32),
        ]
        + [pltpu.VMEM(x, F32) for x in sizes]
        + [pltpu.SemaphoreType.DMA((4, 6)), pltpu.SemaphoreType.DMA((4, 6))],
        compiler_params=pltpu.CompilerParams(vmem_limit_bytes=VMEM_LIMIT),
        name="pack_halos",
    )(tracers, east, north, mask)


def remap_kernel(n_lon, n_lat, src, dst, fold, atm, weights_hbm, out, weights, blocks, edge, labels, count, weight_sem):
    devices = n_lon * n_lat
    sends = weights.shape[0]
    chunks = weight_sem.shape[0]
    per_chunk = sends // chunks

    def weight_copy(i):
        part = pl.ds(i * per_chunk, per_chunk)
        return pltpu.make_async_copy(weights_hbm.at[part], weights.at[part], weight_sem.at[i])

    for i in range(chunks):
        weight_copy(i).start()
    wide = atm[...].astype(F32)
    for b in range(blocks.shape[0]):
        blocks[b, 0:4] = wide[:, b * LANES : (b + 1) * LANES]
    out[...] = jnp.zeros_like(out)
    edge[...] = jnp.zeros_like(edge)
    labels[...] = jnp.zeros_like(labels)

    def clear(i, _):
        count[i] = 0
        return 0

    lax.fori_loop(0, devices, clear, 0, unroll=8)

    lane1 = lanes_of((1, LANES))
    batch = 8

    per = per_chunk // batch

    def chunk(i, _):
        weight_copy(i).wait()
        lax.fori_loop(0, per, lambda j, x: several(i * per + j, x), 0, unroll=per)
        return 0

    def several(i, _):
        places, lefts = [], []
        for j in range(batch):
            w = batch * i + j
            place = dst[w]
            lon = place & (n_lon - 1) if n_lon & (n_lon - 1) == 0 else place % n_lon
            row = place // n_lon
            local = row % ROWS
            owner = lon * n_lat + row // ROWS
            slot = count[owner]
            count[owner] = slot + 1
            kind = jnp.where(local < 2, local, local - (ROWS - 4))
            is_edge = jnp.logical_or(local < 2, local >= ROWS - 2)
            places.append((owner, slot, local, jnp.where(is_edge, owner * 4 + kind, devices * 4)))
            lefts.append(blocks[src[w], 0:4])
        left = jnp.concatenate(lefts, 0).astype(jnp.bfloat16)
        right = weights[pl.ds(pl.multiple_of(batch * i, batch), batch)].reshape(batch * LANES, LANES)
        products = lax.dot_general(left, right, (((1,), (1,)), ((), ())), preferred_element_type=F32)
        for j, (owner, slot, local, at) in enumerate(places):
            product = products[4 * j : 4 * j + 4, LANES * j : LANES * (j + 1)]
            out[owner * GROUPS + slot] = product
            labels[pl.ds(owner, 1)] = jnp.where(lane1 == slot, (local + 1).astype(F32), labels[pl.ds(owner, 1)])
            edge[at] = edge[at] + product
        return 0

    lax.fori_loop(0, chunks, chunk, 0)

    lane4 = lanes_of((4, LANES))
    high = fold[0] // LANES
    low = fold[0] % LANES
    strips = []
    for p in range(n_lon):
        first = edge[(((high - p + 2 * n_lon) % n_lon) * n_lat + n_lat - 1) * 4 + 3]
        second = edge[(((high - p - 1 + 2 * n_lon) % n_lon) * n_lat + n_lat - 1) * 4 + 3]
        strips.append(jnp.where(lane4 <= low, first, second))
    ghost = reversed_lanes(jnp.concatenate(strips, 0), low)
    for owner in range(devices):
        total = jnp.zeros((4, LANES), F32)
        for n in range(4):
            moved = roll(out[owner * GROUPS + n], 2 + 4 * n)
            total = jnp.where(lane4 // 4 == n, moved, total)
        out[owner * GROUPS + 4] = total
    own = labels[...]
    lane = lanes_of(own.shape) - LABEL_LANE
    west = jnp.concatenate([own[devices - n_lat :], own[: devices - n_lat]], 0)
    east = jnp.concatenate([own[n_lat:], own[:n_lat]], 0)
    labels[...] = jnp.where(
        lane < 4, roll(own, LABEL_LANE), jnp.where(lane < 8, roll(west, LABEL_LANE + 4), roll(east, LABEL_LANE + 8))
    )
    for lat in range(n_lat):
        packs = [out[(lon * n_lat + lat) * GROUPS + 4] for lon in range(n_lon)]
        for lon in range(n_lon):
            owner = lon * n_lat + lat
            base = owner * GROUPS
            beside = jnp.where(lane4 < 16, packs[(lon - 1) % n_lon], roll(packs[(lon + 1) % n_lon], 16))
            out[base + 4, 0:3] = beside[0:3]
            out[base + 4, 0:1] = beside[0:1] + labels[owner : owner + 1]
            if lat < n_lat - 1:
                above = (owner + 1) * 4
                out[base + 5, 0:2] = edge[above, 0:2]
                out[base + 5, 2:4] = edge[above + 1, 0:2]
            else:
                out[base + 5, 0:2] = ghost[4 * lon : 4 * lon + 2]
                out[base + 5, 2:4] = ghost[4 * lon : 4 * lon + 2]
            if lat > 0:
                below = (owner - 1) * 4
                out[base + 6, 0:2] = edge[below + 3, 0:2]
                out[base + 6, 2:4] = edge[below + 2, 0:2]
                out[base + 4, 3:4] = edge[below + 3, 3:4]
            else:
                out[base + 4, 3:4] = jnp.zeros((1, LANES), F32)


def reversed_lanes(x, low):
    before = lax.broadcasted_iota(jnp.int32, (LANES, LANES), 0)
    after = lax.broadcasted_iota(jnp.int32, (LANES, LANES), 1)
    table = (before == (low - after + LANES) % LANES).astype(F32)
    return jnp.dot(x, table, precision=lax.Precision.HIGHEST, preferred_element_type=F32)


def remap(atm, weights, src, dst, fold_c, n_lon, n_lat):
    devices = n_lon * n_lat
    blocks = atm.shape[1] // LANES
    smem = pl.BlockSpec(memory_space=pltpu.SMEM)
    return pl.pallas_call(
        functools.partial(remap_kernel, n_lon, n_lat),
        in_specs=[smem, smem, smem, pl.BlockSpec(memory_space=pltpu.VMEM), pl.BlockSpec(memory_space=pltpu.HBM)],
        out_specs=pl.BlockSpec(memory_space=pltpu.VMEM),
        out_shape=jax.ShapeDtypeStruct((devices * GROUPS, 4, LANES), F32),
        scratch_shapes=[
            pltpu.VMEM(weights.shape, weights.dtype),
            pltpu.VMEM((blocks, 8, LANES), F32),
            pltpu.VMEM((devices * 4 + 1, 4, LANES), F32),
            pltpu.VMEM((devices, LANES), F32),
            pltpu.SMEM((devices,), jnp.int32),
            pltpu.SemaphoreType.DMA((8,)),
        ],
        compiler_params=pltpu.CompilerParams(vmem_limit_bytes=VMEM_LIMIT),
        name="remap",
    )(src, dst, fold_c, atm, weights)


def minmod(a, b):
    return jnp.maximum(jnp.minimum(a, b), jnp.minimum(jnp.maximum(a, b), 0.0))


def face_coefficients(flow, mask, drho, zrho):
    diff = DIFFUSIVITY * mask
    strat = 0.25 * zrho
    slope = drho * strat / (strat * strat + SLOPE_EPS)
    up = jnp.maximum(flow, 0.0)
    down = jnp.minimum(flow, 0.0)
    return (
        up + diff,
        down - diff,
        0.5 * up * (1.0 - up),
        -0.5 * down * (1.0 + down),
        0.25 * diff * slope,
    )


def density(temperature, salinity):
    return SALT_BETA_COEFF * salinity - HEAT_ALPHA_COEFF * temperature


def spread(x, lane32):
    for width in (4, 8, 16):
        x = jnp.where(lane32 < width, x, roll(x, width))
    return x


def edge_values(halo, own):
    lane = lanes_of(halo(0, 0).shape)
    lane4, lane32 = lane % 4, lane % 32
    east = lane4 == 0
    parts = []
    for h in range(2):
        p, o = halo(0, h), own(0, h)
        zp, zo = halo(1, h) - halo(-1, h), own(1, h) - own(-1, h)
        o1, p2, zp2 = roll(o, -1), roll(p, -2), roll(zp, -2)
        zo1 = roll(zo, -1)
        parts.append(
            (
                jnp.where(east, o, roll(p, 1)),
                jnp.where(east, o1, p),
                jnp.where(east, p2, o1),
                jnp.where(east, roll(p, -3), roll(o, -2)),
                jnp.where(east, zo1, zp),
                jnp.where(east, zp2, zo1),
            )
        )
    c0, c1, c2, c3, z1, z2 = [jnp.where(lane4 < 2, x, roll(y, 2)) for x, y in zip(*parts)]
    d2 = c2 - c1
    s1, s2 = minmod(d2, c1 - c0), minmod(c3 - c2, d2)
    z = z1 + z2
    mask = roll(c1 * c2, -28)
    coefs = face_coefficients(roll(c1, -24) * mask, mask, density(d2, roll(d2, -4)), density(z, roll(z, -4)))
    a, b, p, q, v = [spread(x, lane32) for x in coefs]
    return jnp.where(lane4 % 2 == 0, s1, s2), a * c1 + b * c2 + p * s1 + q * s2 + v * z


def in_step(*levels):
    levels = list(levels)
    while levels:
        levels = [level for level in levels if next(level, None) is not None]


def level_step(below, cpad, above, rows_below, rows_above, edge_slope, edge_flux, east, north, land, write, scratch):
    zpad, hpad, gpad, slope, xco, yco, mpad, tops = scratch
    lane = lanes_of((8, LANES))
    first_lane, last_lane = lane == 0, lane == LANES - 1
    mid = slice(8, 72)

    below1, below2 = rows_below(0, 1), rows_below(0, 0)
    above1, above2 = rows_above(0, 0), rows_above(0, 1)
    z_below = rows_below(1, 1) - rows_below(-1, 1)
    z_above = rows_above(1, 0) - rows_above(-1, 0)
    for t in range(NTR):
        zpad[t, mid] = above[t, mid] - below[t, mid]
        cpad[t, 7:8] = below1[t : t + 1]
        cpad[t, 72:73] = above1[t : t + 1]
        tops[0, t : t + 1] = cpad[t, 8:9]
        tops[1, t : t + 1] = cpad[t, 71:72]
    for t in range(2):
        zpad[t, 72:73] = z_above[t : t + 1]
    tops[2] = zpad[0, 8:16]
    tops[3] = zpad[1, 8:16]
    mpad[mid] = land
    mpad[72:73] = above1[7:8]

    yield True

    def at_edge(x, r, f):
        return roll(x, -(32 * (r % 4) + 4 * f + 2 * (r // 4) + 1))

    def x_face(t):
        c, z = cpad[t, mid], zpad[t, mid]
        return roll(c, -1) - c, z + roll(z, -1)

    (dt, zt), (ds, zs) = x_face(0), x_face(1)
    mask = land * roll(land, -1)
    a, b, p, q, v = face_coefficients(east * mask, mask, density(dt, ds), density(zt, zs))
    for i, x in enumerate((a, p, v, roll(b, 1), roll(q, 1), roll(v, 1))):
        xco[i] = x
    yield True

    def y_face(t):
        return cpad[t, 9:73] - cpad[t, mid], zpad[t, mid] + zpad[t, 9:73]

    (dt, zt), (ds, zs) = y_face(0), y_face(1)
    mask = land * mpad[9:73]
    for i, x in enumerate(face_coefficients(north * mask, mask, density(dt, ds), density(zt, zs))):
        yco[i, mid] = x
    row0 = tops[0]
    mask = below1[7:8] * mpad[8:9]
    d = row0 - below1
    a, b, p, q, v = face_coefficients(
        below1[6:7] * mask,
        mask,
        density(d[0:1], d[1:2]),
        density(z_below[0:1] + tops[2, 0:1], z_below[1:2] + tops[3, 0:1]),
    )
    yco[1, 7:8], yco[3, 7:8], yco[4, 7:8] = b, q, v
    h_below = a * below1 + p * minmod(d, below1 - below2) + v * z_below
    b, q, v = yco[1, 71:72], yco[3, 71:72], yco[4, 71:72]
    g_above = b * above1 + q * minmod(above2 - above1, above1 - tops[1]) + v * z_above
    for t in range(NTR):
        hpad[t, 7:8] = h_below[t : t + 1]
        gpad[t, 72:73] = g_above[t : t + 1]

    yield True
    at_side = jnp.logical_or(first_lane, last_lane)
    for r in range(8):
        here = slice(8 + 8 * r, 16 + 8 * r)
        lower, upper = slice(7 + 8 * r, 15 + 8 * r), slice(9 + 8 * r, 17 + 8 * r)
        ya, yp, yv, yb, yq, yw = yco[0, here], yco[2, here], yco[4, here], yco[1, lower], yco[3, lower], yco[4, lower]
        for t in range(NTR):
            c, z = cpad[t, here], zpad[t, here]
            s = minmod(roll(c, -1) - c, c - roll(c, 1))
            slope[t, 8 * r : 8 * r + 8] = jnp.where(at_side, at_edge(edge_slope, r, t), s)
            s = minmod(cpad[t, upper] - c, c - cpad[t, lower])
            hpad[t, here] = ya * c + yp * s + yv * z
            gpad[t, here] = yb * c + yq * s + yw * z
        yield True
    for r in range(8):
        here = slice(8 + 8 * r, 16 + 8 * r)
        lower, upper = slice(7 + 8 * r, 15 + 8 * r), slice(9 + 8 * r, 17 + 8 * r)
        part = slice(8 * r, 8 * r + 8)
        xa, xp, xv, xb, xq, xw = [xco[i, part] for i in range(6)]
        wet = mpad[here]
        for t in range(NTR):
            c, z, s = cpad[t, here], zpad[t, here], slope[t, part]
            h = xa * c + xp * s + xv * z
            g = xb * c + xq * s + xw * z
            flux = at_edge(edge_flux, r, t)
            out_east = jnp.where(last_lane, flux, h + roll(g, -1))
            in_west = jnp.where(first_lane, flux, g + roll(h, 1))
            out_north = hpad[t, here] + gpad[t, upper]
            in_south = hpad[t, lower] + gpad[t, here]
            write(t, part, wet * (c - (out_east - in_west) - (out_north - in_south)))
        yield True


def level_scratch():
    padded = pltpu.VMEM((NTR, 80, LANES), F32)
    return [
        padded,
        padded,
        padded,
        pltpu.VMEM((NTR, ROWS, LANES), F32),
        pltpu.VMEM((6, ROWS, LANES), F32),
        pltpu.VMEM((5, 80, LANES), F32),
        pltpu.VMEM((80, LANES), F32),
        pltpu.VMEM((4, 8, LANES), F32),
    ]


def chunk_spans(lo, hi):
    spans, size = [], 4
    while lo < hi:
        end = min(lo + size, hi)
        if hi - end < size:
            end = hi
        spans.append((lo, end))
        lo, size = end, size + 2
    return spans


def deep_kernel(
    first, together, top, tracers, east, north, mask, west_cols, east_cols, own_cols, row_below, row_above, ghost, out,
    cells, flows_e, flows_n, lands, west_v, east_v, own_v, below_v, above_v, ghost_v, results, edges, halo_sem, level_sem, out_sem, *scratch
):
    levels = cells.shape[1]

    def halo_copies():
        pairs = ((row_below, below_v), (row_above, above_v), (west_cols, west_v), (east_cols, east_v), (own_cols, own_v), (ghost, ghost_v))
        return [pltpu.make_async_copy(a, b, halo_sem.at[i]) for i, (a, b) in enumerate(pairs)]

    spans = chunk_spans(first - 1, levels)
    sends = chunk_spans(first, levels)[::-1]
    sends = [(first + levels - hi, first + levels - lo) for lo, hi in sends]

    def cell_copy(i):
        lo, hi = spans[i]
        return pltpu.make_async_copy(tracers.at[:, lo:hi], cells.at[:, lo:hi, 8:72], level_sem.at[0, i])

    def flow_copies(i):
        lo, hi = spans[i]
        pairs = ((east, flows_e), (north, flows_n), (mask, lands))
        return [pltpu.make_async_copy(a.at[lo:hi], b.at[lo:hi], level_sem.at[1 + j, i]) for j, (a, b) in enumerate(pairs)]

    def out_copy(i):
        lo, hi = sends[i]
        return pltpu.make_async_copy(results.at[:, lo - first : hi - first], out.at[:, lo:hi], out_sem.at[i])

    cell_copy(0).start()
    for copy in flow_copies(0) + halo_copies():
        copy.start()
    for i in range(1, len(spans)):
        cell_copy(i).start()
        for copy in flow_copies(i):
            copy.start()
    for copy in halo_copies():
        copy.wait()

    @pl.when(top[0] > 0)
    def _():
        field = lax.broadcasted_iota(jnp.int32, ghost_v.shape, 1)
        above_v[:, 0] = jnp.where(field == 7, 1.0, ghost_v[...])
        above_v[:, 1] = ghost_v[...]

    for lo in range(first, levels, EDGE_LEVELS):
        ks = range(lo, min(lo + EDGE_LEVELS, levels))
        stacked = (8 * len(ks), LANES)
        lane_of_four = lanes_of(stacked) % 4

        def stack(ref, j, h):
            return jnp.concatenate([ref[min(k + j, levels - 1), h] for k in ks], 0)

        slopes, fluxes = edge_values(
            lambda j, h: jnp.where(lane_of_four < 2, stack(west_v, j, h), stack(east_v, j, h)),
            lambda j, h: stack(own_v, j, h),
        )
        for i, k in enumerate(ks):
            edges[k, 0] = slopes[8 * i : 8 * i + 8]
            edges[k, 1] = fluxes[8 * i : 8 * i + 8]
    for copy in flow_copies(0) + [cell_copy(0)]:
        copy.wait()

    def several(i, _):
        k0 = first + i * together
        for i in range(1, len(spans)):

            @pl.when(jnp.logical_and(k0 + together >= spans[i][0], k0 < spans[i][0]))
            def _():
                for copy in flow_copies(i) + [cell_copy(i)]:
                    copy.wait()

        size = len(scratch) // together
        in_step(*[one(k0 + j, scratch[j * size : (j + 1) * size]) for j in range(together)])
        for i in range(len(sends)):

            @pl.when(k0 + together == sends[i][1])
            def _():
                out_copy(i).start()

        return 0

    def one(k, scratch):
        level = {-1: k - 1, 0: k, 1: jnp.minimum(k + 1, levels - 1)}

        def write(t, part, value):
            results[t, k - first, part] = value

        return level_step(
            cells.at[:, k - 1],
            cells.at[:, k],
            cells.at[:, level[1]],
            lambda j, i: below_v[level[j], i],
            lambda j, i: above_v[level[j], i],
            edges[k, 0],
            edges[k, 1],
            flows_e[k],
            flows_n[k],
            lands[k].astype(F32),
            write,
            scratch,
        )

    lax.fori_loop(0, (levels - first) // together, several, 0)
    for i in range(len(sends)):
        out_copy(i).wait()


def deep_levels(first, top, tracers, east, north, mask, west_cols, east_cols, own_cols, row_below, row_above, ghost):
    levels = tracers.shape[1]
    halos = (west_cols, east_cols, own_cols, row_below, row_above, ghost)
    flow = (levels, ROWS, LANES)
    return pl.pallas_call(
        functools.partial(deep_kernel, first, TOGETHER),
        in_specs=[pl.BlockSpec(memory_space=pltpu.SMEM)]
        + [pl.BlockSpec(memory_space=pltpu.HBM)] * 4
        + [pl.BlockSpec(memory_space=pl.ANY)] * 6,
        out_specs=pl.BlockSpec(memory_space=pl.ANY),
        out_shape=jax.ShapeDtypeStruct(tracers.shape, F32),
        scratch_shapes=[
            pltpu.VMEM((NTR, levels, ROWS + 16, LANES), F32),
            pltpu.VMEM(flow, F32),
            pltpu.VMEM(flow, F32),
            pltpu.VMEM(flow, jnp.int32),
        ]
        + [pltpu.VMEM(x.shape, F32) for x in halos]
        + [
            pltpu.VMEM((NTR, levels - first, ROWS, LANES), F32),
            pltpu.VMEM((levels, 2, 8, LANES), F32),
            pltpu.SemaphoreType.DMA((6,)),
            pltpu.SemaphoreType.DMA((4, levels)),
            pltpu.SemaphoreType.DMA((levels,)),
        ]
        + level_scratch() * TOGETHER,
        compiler_params=pltpu.CompilerParams(vmem_limit_bytes=VMEM_LIMIT),
        name="deep_levels",
    )(top, tracers, east, north, mask, *halos)


def expand(x, lane):
    total = x
    for f in range(2, 6):
        total = jnp.where(lane // 4 == f, roll(x, 4 * (f - 1)), total)
    return jnp.where(lane // 4 == 6, roll(x, 16), total)


def pack_rows(tiles, lane):
    packed = []
    for h in range(2):
        total = jnp.zeros((8, LANES), F32)
        for rr in range(4):
            total = jnp.where(lane // 32 == rr, roll(tiles[4 * h + rr], 32 * rr), total)
        packed.append(total)
    return packed


def force_columns(cols, force, lane):
    field = (lane % 32) // 4
    mask = spread(roll(cols, -28), lane % 32)
    tracer_change = mask * (force * jnp.where(field == 0, HEAT_SCALE, FRESH_SCALE * cols))
    return cols + jnp.where(field < 6, tracer_change, jnp.where(field == 6, STRESS_SCALE * force, 0.0))


def force_rows(rows, mask, heat, fresh, tau):
    field = lax.broadcasted_iota(jnp.int32, (8, LANES), 0)
    tracer_change = mask * jnp.where(field == 0, HEAT_SCALE * heat, FRESH_SCALE * fresh * rows)
    return rows + jnp.where(field < 6, tracer_change, jnp.where(field == 6, STRESS_SCALE * tau, 0.0))


def surface_kernel(
    top, arrived, tracers, east, north, mask, west_cols, east_cols, own_cols, row_below, arriving_above, ghost, _, forcing, out,
    row_above, cells, cell_sem, rows_b, rows_a, cols_h, cols_o, *scratch
):
    copy = pltpu.make_async_copy(tracers.at[:, 0:3], cells.at[:, :, 8:72], cell_sem)
    copy.start()
    devices = arrived.shape[0] // (4 * GROUPS)
    stride = 4 * GROUPS
    lane = lanes_of((8, LANES))
    lane_of_four = lane % 4

    def gathered(group, row):
        return arrived[pl.ds(4 * group + row, devices, stride=stride), :]

    labels = gathered(4, 0).T[LABEL_LANE : LABEL_LANE + 16]
    row_id = lax.broadcasted_iota(jnp.int32, (ROWS, devices), 0).astype(F32) + 1.0

    def pick(n):
        return (labels[n : n + 1] == row_id).astype(F32)

    def dot(a, b):
        return jnp.dot(a, b, precision=lax.Precision.HIGHEST, preferred_element_type=F32)

    flux = jnp.zeros((ROWS, 4 * LANES), F32)
    for n in range(4):
        flux += dot(pick(n), jnp.concatenate([gathered(n, f) for f in range(4)], 1))
    fields = [flux[:, LANES * f : LANES * (f + 1)] for f in range(4)]
    for f in range(4):
        forcing[f] = fields[f]
    heat, fresh, tau_x, tau_y = fields

    wide = lanes_of((devices, LANES))
    sides = [gathered(4, f) for f in range(3)]
    beside = jnp.zeros((ROWS, LANES), F32)
    for side in range(2):
        for n in range(4):
            back = -4 * n - 16 * side
            lined = jnp.where(
                wide < 4, roll(sides[0], back), jnp.where(wide < 8, roll(sides[1], back + 4), roll(sides[2], back + 8))
            )
            lined = jnp.where((wide < 12) & (wide % 4 // 2 == side), lined, 0.0)
            beside += dot(pick(4 + 4 * side + n), lined)

    over = [jnp.sum(gathered(5, f), 0, keepdims=True) for f in range(4)]
    under = [jnp.sum(gathered(6, f), 0, keepdims=True) for f in range(4)]
    tau_under = jnp.sum(gathered(4, 3), 0, keepdims=True)
    is_top = top[0] > 0
    field = lax.broadcasted_iota(jnp.int32, (8, LANES), 0)
    for k in range(3):
        row_above[k, 0] = jnp.where(is_top, jnp.where(field == 7, 1.0, ghost[k]), arriving_above[k, 0])
        row_above[k, 1] = jnp.where(is_top, ghost[k], arriving_above[k, 1])

    land = [mask[k].astype(F32) for k in range(2)]
    copy.wait()
    cells[0, 0, 8:72] = cells[0, 0, 8:72] + land[0] * (HEAT_SCALE * heat)
    for t in range(1, NTR):
        c = cells[t, 0, 8:72]
        cells[t, 0, 8:72] = c + land[0] * (FRESH_SCALE * fresh * c)
    rows_b[0] = force_rows(row_below[0, 0], row_below[0, 0, 7:8], under[2], under[3], 0.0)
    rows_b[1] = force_rows(row_below[0, 1], row_below[0, 1, 7:8], under[0], under[1], tau_under)
    near = jnp.where(is_top, row_above[0, 1, 7:8], row_above[0, 0, 7:8])
    rows_a[0] = force_rows(row_above[0, 0], near, over[0], over[1], 0.0)
    rows_a[1] = force_rows(row_above[0, 1], row_above[0, 1, 7:8], over[2], over[3], 0.0)
    own_tiles, halo_tiles = [], []
    for r in range(8):
        part = slice(8 * r, 8 * r + 8)
        mine = jnp.where(lane < 4, roll(heat[part], 2), jnp.where(lane < 8, roll(fresh[part], 6), roll(tau_x[part], 10)))
        own_tiles.append(expand(mine, lane))
        halo_tiles.append(expand(beside[part], lane))
    own_force, halo_force = pack_rows(own_tiles, lane), pack_rows(halo_tiles, lane)
    for h in range(2):
        cols = jnp.where(lane_of_four < 2, west_cols[0, h], east_cols[0, h])
        cols_h[h] = force_columns(cols, halo_force[h], lane)
        cols_o[h] = force_columns(own_cols[0, h], own_force[h], lane)

    def level(k):
        def at(j):
            return max(k + j, 0)

        def write(t, part, value):
            out[t, k, part] = value

        size = len(scratch) // 2
        return level_step(
            cells.at[:, at(-1)],
            cells.at[:, k],
            cells.at[:, k + 1],
            lambda j, i: rows_b[i] if at(j) == 0 else row_below[at(j), i],
            lambda j, i: rows_a[i] if at(j) == 0 else row_above[at(j), i],
            slopes[8 * k : 8 * k + 8],
            fluxes[8 * k : 8 * k + 8],
            east[k] + STRESS_SCALE * tau_x if k == 0 else east[k],
            north[k] + STRESS_SCALE * tau_y if k == 0 else north[k],
            land[k],
            write,
            scratch[size * k : size * (k + 1)],
        )

    def halo_at(k, h):
        return cols_h[h] if k <= 0 else jnp.where(lane_of_four < 2, west_cols[k, h], east_cols[k, h])

    def own_at(k, h):
        return cols_o[h] if k <= 0 else own_cols[k, h]

    slopes, fluxes = edge_values(
        lambda j, h: jnp.concatenate([halo_at(k + j, h) for k in range(2)], 0),
        lambda j, h: jnp.concatenate([own_at(k + j, h) for k in range(2)], 0),
    )
    in_step(level(0), level(1))


def surface_levels(top, arrived, tracers, east, north, mask, west_cols, east_cols, own_cols, row_below, row_above, ghost, done):
    block = lambda n: pl.BlockSpec((NTR, n, ROWS, LANES), lambda i: (0, 0, 0, 0))
    flow = pl.BlockSpec((2, ROWS, LANES), lambda i: (0, 0, 0))
    halo = lambda x: pl.BlockSpec((3,) + x.shape[1:], lambda i: (0,) * x.ndim)
    return pl.pallas_call(
        surface_kernel,
        grid=(1,),
        in_specs=[
            pl.BlockSpec(memory_space=pltpu.SMEM),
            pl.BlockSpec(arrived.shape, lambda i: (0, 0)),
            pl.BlockSpec(memory_space=pltpu.HBM),
            flow,
            flow,
            flow,
        ]
        + [halo(x) for x in (west_cols, east_cols, own_cols, row_below, row_above, ghost)]
        + [pl.BlockSpec(memory_space=pltpu.HBM)],
        out_specs=[pl.BlockSpec((4, ROWS, LANES), lambda i: (0, 0, 0)), block(2)],
        out_shape=[jax.ShapeDtypeStruct((4, ROWS, LANES), F32), jax.ShapeDtypeStruct(tracers.shape, F32)],
        input_output_aliases={12: 1},
        scratch_shapes=[
            pltpu.VMEM((3, 2, 8, LANES), F32),
            pltpu.VMEM((NTR, 3, ROWS + 16, LANES), F32),
            pltpu.SemaphoreType.DMA,
            pltpu.VMEM((2, 8, LANES), F32),
            pltpu.VMEM((2, 8, LANES), F32),
            pltpu.VMEM((2, 8, LANES), F32),
            pltpu.VMEM((2, 8, LANES), F32),
        ]
        + level_scratch() * 2,
        compiler_params=pltpu.CompilerParams(vmem_limit_bytes=VMEM_LIMIT),
        name="surface_levels",
    )(top, arrived, tracers, east, north, mask, west_cols, east_cols, own_cols, row_below, row_above, ghost, done)


def strip_kernel(c, own, west, out):
    low = c[0] % LANES
    levels = own.shape[0]
    lane = lanes_of((levels, 8, LANES))
    joined = jnp.where(lane <= low, own[:, 0], west[:, 0]).reshape(levels * 8, LANES)
    out[...] = reversed_lanes(joined, low).reshape(levels, 8, LANES)


def fold_strip(both, west_cols, c):
    levels = both.shape[0]
    top = pl.BlockSpec((levels, 1, 8, LANES), lambda i: (0, 2, 0, 0))
    return pl.pallas_call(
        strip_kernel,
        grid=(1,),
        in_specs=[pl.BlockSpec(memory_space=pltpu.SMEM), top, top],
        out_specs=pl.BlockSpec((levels, 8, LANES), lambda i: (0, 0, 0)),
        out_shape=jax.ShapeDtypeStruct((levels, 8, LANES), F32),
        name="fold_strip",
    )(c, both, west_cols)


def body(tracers, flow_east, flow_north, sea_mask, atm_fields, remap_weights, remap_src, remap_dst, fold_partner):
    n_lon, n_lat = lax.axis_size("lon"), lax.axis_size("lat")
    devices = n_lon * n_lat
    lon, lat = lax.axis_index("lon"), lax.axis_index("lat")
    c = (fold_partner[0] + lon * LANES) % (n_lon * LANES)
    top = (lat == n_lat - 1).astype(jnp.int32)[None]

    both, own_cols, up, down = pack_halos(tracers, flow_east, flow_north, sea_mask)
    right = [(i, (i + 1) % n_lon) for i in range(n_lon)]
    left = [(j, i) for i, j in right]
    north = [(i, i + 1) for i in range(n_lat - 1)]
    south = [(j, i) for i, j in north]
    west_cols = lax.ppermute(both, "lon", right)
    row_below = lax.ppermute(up, "lat", north)
    row_above = lax.ppermute(down, "lat", south)
    east_cols = lax.ppermute(own_cols, "lon", left)
    atm_fields, _ = lax.optimization_barrier((atm_fields, both))
    outgoing = remap(atm_fields, remap_weights, remap_src, remap_dst, c[None], n_lon, n_lat)
    west_cols, outgoing = lax.optimization_barrier((west_cols, outgoing))
    strip = fold_strip(both, west_cols, c[None])

    def move(b):
        pairs = [(q * n_lat + n_lat - 1, ((b - q) % n_lon) * n_lat + n_lat - 1) for q in range(n_lon)]
        return lambda x: lax.ppermute(x, ("lon", "lat"), pairs)

    ghost = lax.switch(c // LANES, [move(b) for b in range(n_lon)], strip)
    outgoing, ghost, east_cols, row_below, row_above = lax.optimization_barrier(
        (outgoing, ghost, east_cols, row_below, row_above)
    )
    arrived = lax.all_to_all(outgoing, ("lon", "lat"), split_axis=0, concat_axis=0, tiled=True)
    halos = (west_cols, east_cols, own_cols, row_below, row_above, ghost)
    done = deep_levels(2, top, tracers, flow_east, flow_north, sea_mask, *halos)
    arrived = arrived.reshape(devices * 4 * GROUPS, LANES)
    return surface_levels(top, arrived, tracers, flow_east, flow_north, sea_mask, *halos, done)


def solution(mesh):
    placed = (
        P(None, None, "lat", "lon"),
        P(None, "lat", "lon"),
        P(None, "lat", "lon"),
        P(None, "lat", "lon"),
        P(None, ("lon", "lat")),
        P(("lon", "lat"), None, None),
        P(("lon", "lat")),
        P(("lon", "lat")),
        P("lon"),
    )
    return jax.shard_map(
        body,
        mesh=mesh,
        in_specs=placed,
        out_specs=(P(None, "lat", "lon"), P(None, None, "lat", "lon")),
        check_vma=False,
    )
```

```python
import functools

import jax
import jax.numpy as jnp
from jax import lax
from jax.experimental import pallas as pl
from jax.experimental.pallas import tpu as pltpu
from jax.sharding import PartitionSpec as P

HEAT_SCALE = 0.1
FRESH_SCALE = 0.03
STRESS_SCALE = 0.02
HEAT_ALPHA_COEFF = 0.2
SALT_BETA_COEFF = 0.8
SLOPE_EPS = 0.5
DIFFUSIVITY = 0.1

NTR = 6
ROWS = 64
LANES = 128
GROUPS = 7
LABEL_LANE = 32
F32 = jnp.float32
TOGETHER = 2
EDGE_LEVELS = 8
VMEM_LIMIT = 56 * 1024 * 1024


def roll(x, shift):
    return pltpu.roll(x, shift % LANES, axis=1)


def lanes_of(shape):
    return lax.broadcasted_iota(jnp.int32, shape, len(shape) - 1)


def pack_kernel(
    tracers, east, north, mask, both_out, cols_out, up_out, down_out,
    cells, flows_e, flows_n, lands, both_ref, cols_ref, up_ref, down_ref, in_sem, out_sem
):
    lane_group = lanes_of((8, LANES)) // 4
    levels = east.shape[0]
    step = 4
    chunks = levels // step

    def in_copies(i):
        part = pl.ds(i * step, step)
        pairs = ((east, flows_e), (north, flows_n), (mask, lands))
        copies = [pltpu.make_async_copy(a.at[part], b.at[part], in_sem.at[j, i]) for j, (a, b) in enumerate(pairs)]
        return copies + [pltpu.make_async_copy(tracers.at[:, part], cells.at[:, part], in_sem.at[3, i])]

    def out_copies(i):
        part = pl.ds(i * step, step)
        pairs = ((both_ref, both_out), (cols_ref, cols_out), (up_ref, up_out), (down_ref, down_out))
        return [pltpu.make_async_copy(a.at[part], b.at[part], out_sem.at[j, i]) for j, (a, b) in enumerate(pairs)]

    for i in range(chunks):
        for copy in in_copies(i):
            copy.start()

    def chunk(i, _):
        for copy in in_copies(i):
            copy.wait()
        for j in range(step):
            one(i * step + j)
        for copy in out_copies(i):
            copy.start()
        return 0

    def one(k):
        land = lands[k].astype(F32)
        for h in range(2):
            total = jnp.zeros((8, LANES), F32)
            for rr in range(4):
                start = (4 * h + rr) * 8
                for f in range(8):
                    if f < NTR:
                        tile = cells[f, k, start : start + 8]
                    else:
                        tile = land[start : start + 8] if f == 7 else flows_e[k, start : start + 8]
                    moved = roll(tile, 2 + 32 * rr + 4 * f)
                    total = jnp.where(lane_group == 8 * rr + f, moved, total)
            both_ref[k, h] = total
            cols_ref[k, h] = total

        def row(f, r):
            if f < NTR:
                return cells[f, k, r : r + 1]
            return land[r : r + 1] if f == 7 else flows_n[k, r : r + 1]

        for f in range(8):
            last = row(f, ROWS - 1)
            both_ref[k, 2, f : f + 1] = last
            up_ref[k, 0, f : f + 1] = row(f, ROWS - 2)
            up_ref[k, 1, f : f + 1] = last
            for i in range(2):
                down_ref[k, i, f : f + 1] = row(f, i)

    lax.fori_loop(0, chunks, chunk, 0)
    for i in range(chunks):
        for copy in out_copies(i):
            copy.wait()


def pack_halos(tracers, east, north, mask):
    levels = east.shape[0]
    sizes = [(levels, n, 8, LANES) for n in (3, 2, 2, 2)]
    flow = (levels, ROWS, LANES)
    return pl.pallas_call(
        pack_kernel,
        in_specs=[pl.BlockSpec(memory_space=pltpu.HBM)] * 4,
        out_specs=[pl.BlockSpec(memory_space=pl.ANY)] * 4,
        out_shape=[jax.ShapeDtypeStruct(x, F32) for x in sizes],
        scratch_shapes=[
            pltpu.VMEM(tracers.shape, F32),
            pltpu.VMEM(flow, F32),
            pltpu.VMEM(flow, F32),
            pltpu.VMEM(flow, jnp.int32),
        ]
        + [pltpu.VMEM(x, F32) for x in sizes]
        + [pltpu.SemaphoreType.DMA((4, 6)), pltpu.SemaphoreType.DMA((4, 6))],
        compiler_params=pltpu.CompilerParams(vmem_limit_bytes=VMEM_LIMIT),
        name="pack_halos",
    )(tracers, east, north, mask)


def parts_of(x, size):
    assert size & (size - 1) == 0
    return lax.shift_right_logical(x, size.bit_length() - 1), x & (size - 1)


def remap_kernel(n_lon, n_lat, src, dst, fold, atm, weights_hbm, out, weights, blocks, edge, labels, count, weight_sem):
    devices = n_lon * n_lat
    sends = weights.shape[0]
    chunks = weight_sem.shape[0]
    per_chunk = sends // chunks

    def weight_copy(i):
        part = pl.ds(i * per_chunk, per_chunk)
        return pltpu.make_async_copy(weights_hbm.at[part], weights.at[part], weight_sem.at[i])

    for i in range(chunks):
        weight_copy(i).start()
    wide = atm[...].astype(F32)
    for b in range(blocks.shape[0]):
        blocks[b, 0:4] = wide[:, b * LANES : (b + 1) * LANES]
    out[...] = jnp.zeros_like(out)
    edge[...] = jnp.zeros_like(edge)
    labels[...] = jnp.zeros_like(labels)

    def clear(i, _):
        count[i] = 0
        return 0

    lax.fori_loop(0, devices, clear, 0, unroll=8)

    lane1 = lanes_of((1, LANES))
    batch = 8

    per = per_chunk // batch

    def chunk(i, _):
        weight_copy(i).wait()
        lax.fori_loop(0, per, lambda j, x: several(i * per + j, x), 0, unroll=per)
        return 0

    def several(i, _):
        places, lefts = [], []
        for j in range(batch):
            w = batch * i + j
            place = dst[w]
            row, lon = parts_of(place, n_lon)
            lat, local = parts_of(row, ROWS)
            owner = lon * n_lat + lat
            slot = count[owner]
            count[owner] = slot + 1
            is_edge = ((local + 2) & (ROWS - 1)) < 4
            places.append((owner, slot, local, jnp.where(is_edge, owner * 4 + (local & 3), devices * 4)))
            lefts.append(blocks[src[w], 0:4])
        left = jnp.concatenate(lefts, 0).astype(jnp.bfloat16)
        right = weights[pl.ds(pl.multiple_of(batch * i, batch), batch)].reshape(batch * LANES, LANES)
        products = lax.dot_general(left, right, (((1,), (1,)), ((), ())), preferred_element_type=F32)
        for j, (owner, slot, local, at) in enumerate(places):
            product = products[4 * j : 4 * j + 4, LANES * j : LANES * (j + 1)]
            out[owner * GROUPS + slot] = product
            labels[pl.ds(owner, 1)] = jnp.where(lane1 == slot, (local + 1).astype(F32), labels[pl.ds(owner, 1)])
            edge[at] = edge[at] + product
        return 0

    lax.fori_loop(0, chunks, chunk, 0)

    lane4 = lanes_of((4, LANES))
    high = fold[0] // LANES
    low = fold[0] % LANES
    strips = []
    for p in range(n_lon):
        first = edge[(((high - p + 2 * n_lon) % n_lon) * n_lat + n_lat - 1) * 4 + 3]
        second = edge[(((high - p - 1 + 2 * n_lon) % n_lon) * n_lat + n_lat - 1) * 4 + 3]
        strips.append(jnp.where(lane4 <= low, first, second))
    ghost = reversed_lanes(jnp.concatenate(strips, 0), low)
    for owner in range(devices):
        total = jnp.zeros((4, LANES), F32)
        for n in range(4):
            moved = roll(out[owner * GROUPS + n], 2 + 4 * n)
            total = jnp.where(lane4 // 4 == n, moved, total)
        out[owner * GROUPS + 4] = total
    own = labels[...]
    lane = lanes_of(own.shape) - LABEL_LANE
    west = jnp.concatenate([own[devices - n_lat :], own[: devices - n_lat]], 0)
    east = jnp.concatenate([own[n_lat:], own[:n_lat]], 0)
    labels[...] = jnp.where(
        lane < 4, roll(own, LABEL_LANE), jnp.where(lane < 8, roll(west, LABEL_LANE + 4), roll(east, LABEL_LANE + 8))
    )
    for lat in range(n_lat):
        packs = [out[(lon * n_lat + lat) * GROUPS + 4] for lon in range(n_lon)]
        for lon in range(n_lon):
            owner = lon * n_lat + lat
            base = owner * GROUPS
            beside = jnp.where(lane4 < 16, packs[(lon - 1) % n_lon], roll(packs[(lon + 1) % n_lon], 16))
            out[base + 4, 0:3] = beside[0:3]
            out[base + 4, 0:1] = beside[0:1] + labels[owner : owner + 1]
            if lat < n_lat - 1:
                above = (owner + 1) * 4
                out[base + 5, 0:2] = edge[above, 0:2]
                out[base + 5, 2:4] = edge[above + 1, 0:2]
            else:
                out[base + 5, 0:2] = ghost[4 * lon : 4 * lon + 2]
                out[base + 5, 2:4] = ghost[4 * lon : 4 * lon + 2]
            if lat > 0:
                below = (owner - 1) * 4
                out[base + 6, 0:2] = edge[below + 3, 0:2]
                out[base + 6, 2:4] = edge[below + 2, 0:2]
                out[base + 4, 3:4] = edge[below + 3, 3:4]
            else:
                out[base + 4, 3:4] = jnp.zeros((1, LANES), F32)


def reversed_lanes(x, low):
    before = lax.broadcasted_iota(jnp.int32, (LANES, LANES), 0)
    after = lax.broadcasted_iota(jnp.int32, (LANES, LANES), 1)
    table = (before == (low - after + LANES) % LANES).astype(F32)
    return jnp.dot(x, table, precision=lax.Precision.HIGHEST, preferred_element_type=F32)


def remap(atm, weights, src, dst, fold_c, n_lon, n_lat):
    devices = n_lon * n_lat
    blocks = atm.shape[1] // LANES
    smem = pl.BlockSpec(memory_space=pltpu.SMEM)
    return pl.pallas_call(
        functools.partial(remap_kernel, n_lon, n_lat),
        in_specs=[smem, smem, smem, pl.BlockSpec(memory_space=pltpu.VMEM), pl.BlockSpec(memory_space=pltpu.HBM)],
        out_specs=pl.BlockSpec(memory_space=pltpu.VMEM),
        out_shape=jax.ShapeDtypeStruct((devices * GROUPS, 4, LANES), F32),
        scratch_shapes=[
            pltpu.VMEM(weights.shape, weights.dtype),
            pltpu.VMEM((blocks, 8, LANES), F32),
            pltpu.VMEM((devices * 4 + 1, 4, LANES), F32),
            pltpu.VMEM((devices, LANES), F32),
            pltpu.SMEM((devices,), jnp.int32),
            pltpu.SemaphoreType.DMA((8,)),
        ],
        compiler_params=pltpu.CompilerParams(vmem_limit_bytes=VMEM_LIMIT),
        name="remap",
    )(src, dst, fold_c, atm, weights)


def minmod(a, b):
    return jnp.maximum(jnp.minimum(a, b), jnp.minimum(jnp.maximum(a, b), 0.0))


def face_coefficients(flow, mask, drho, zrho):
    diff = DIFFUSIVITY * mask
    strat = 0.25 * zrho
    slope = drho * strat / (strat * strat + SLOPE_EPS)
    up = jnp.maximum(flow, 0.0)
    down = jnp.minimum(flow, 0.0)
    return (
        up + diff,
        down - diff,
        0.5 * up * (1.0 - up),
        -0.5 * down * (1.0 + down),
        0.25 * diff * slope,
    )


def density(temperature, salinity):
    return SALT_BETA_COEFF * salinity - HEAT_ALPHA_COEFF * temperature


def spread(x, lane32):
    for width in (4, 8, 16):
        x = jnp.where(lane32 < width, x, roll(x, width))
    return x


def edge_values(halo, own):
    lane = lanes_of(halo(0, 0).shape)
    lane4, lane32 = lane % 4, lane % 32
    east = lane4 == 0
    parts = []
    for h in range(2):
        p, o = halo(0, h), own(0, h)
        zp, zo = halo(1, h) - halo(-1, h), own(1, h) - own(-1, h)
        o1, p2, zp2 = roll(o, -1), roll(p, -2), roll(zp, -2)
        zo1 = roll(zo, -1)
        parts.append(
            (
                jnp.where(east, o, roll(p, 1)),
                jnp.where(east, o1, p),
                jnp.where(east, p2, o1),
                jnp.where(east, roll(p, -3), roll(o, -2)),
                jnp.where(east, zo1, zp),
                jnp.where(east, zp2, zo1),
            )
        )
    c0, c1, c2, c3, z1, z2 = [jnp.where(lane4 < 2, x, roll(y, 2)) for x, y in zip(*parts)]
    d2 = c2 - c1
    s1, s2 = minmod(d2, c1 - c0), minmod(c3 - c2, d2)
    z = z1 + z2
    mask = roll(c1 * c2, -28)
    coefs = face_coefficients(roll(c1, -24) * mask, mask, density(d2, roll(d2, -4)), density(z, roll(z, -4)))
    a, b, p, q, v = [spread(x, lane32) for x in coefs]
    return jnp.where(lane4 % 2 == 0, s1, s2), a * c1 + b * c2 + p * s1 + q * s2 + v * z


def in_step(*levels):
    levels = list(levels)
    while levels:
        levels = [level for level in levels if next(level, None) is not None]


def level_step(below, cpad, above, rows_below, rows_above, edge_slope, edge_flux, east, north, land, write, scratch):
    zpad, hpad, gpad, slope, xco, yco, mpad, tops = scratch
    lane = lanes_of((8, LANES))
    first_lane, last_lane = lane == 0, lane == LANES - 1
    mid = slice(8, 72)

    below1, below2 = rows_below(0, 1), rows_below(0, 0)
    above1, above2 = rows_above(0, 0), rows_above(0, 1)
    z_below = rows_below(1, 1) - rows_below(-1, 1)
    z_above = rows_above(1, 0) - rows_above(-1, 0)
    for t in range(NTR):
        zpad[t, mid] = above[t, mid] - below[t, mid]
        cpad[t, 7:8] = below1[t : t + 1]
        cpad[t, 72:73] = above1[t : t + 1]
        tops[0, t : t + 1] = cpad[t, 8:9]
        tops[1, t : t + 1] = cpad[t, 71:72]
    for t in range(2):
        zpad[t, 72:73] = z_above[t : t + 1]
    tops[2] = zpad[0, 8:16]
    tops[3] = zpad[1, 8:16]
    mpad[mid] = land
    mpad[72:73] = above1[7:8]

    yield True

    def at_edge(x, r, f):
        return roll(x, -(32 * (r % 4) + 4 * f + 2 * (r // 4) + 1))

    def x_face(t):
        c, z = cpad[t, mid], zpad[t, mid]
        return roll(c, -1) - c, z + roll(z, -1)

    (dt, zt), (ds, zs) = x_face(0), x_face(1)
    mask = land * roll(land, -1)
    a, b, p, q, v = face_coefficients(east * mask, mask, density(dt, ds), density(zt, zs))
    for i, x in enumerate((a, p, v, roll(b, 1), roll(q, 1), roll(v, 1))):
        xco[i] = x
    yield True

    def y_face(t):
        return cpad[t, 9:73] - cpad[t, mid], zpad[t, mid] + zpad[t, 9:73]

    (dt, zt), (ds, zs) = y_face(0), y_face(1)
    mask = land * mpad[9:73]
    for i, x in enumerate(face_coefficients(north * mask, mask, density(dt, ds), density(zt, zs))):
        yco[i, mid] = x
    row0 = tops[0]
    mask = below1[7:8] * mpad[8:9]
    d = row0 - below1
    a, b, p, q, v = face_coefficients(
        below1[6:7] * mask,
        mask,
        density(d[0:1], d[1:2]),
        density(z_below[0:1] + tops[2, 0:1], z_below[1:2] + tops[3, 0:1]),
    )
    yco[1, 7:8], yco[3, 7:8], yco[4, 7:8] = b, q, v
    h_below = a * below1 + p * minmod(d, below1 - below2) + v * z_below
    b, q, v = yco[1, 71:72], yco[3, 71:72], yco[4, 71:72]
    g_above = b * above1 + q * minmod(above2 - above1, above1 - tops[1]) + v * z_above
    for t in range(NTR):
        hpad[t, 7:8] = h_below[t : t + 1]
        gpad[t, 72:73] = g_above[t : t + 1]

    yield True
    at_side = jnp.logical_or(first_lane, last_lane)
    for r in range(8):
        here = slice(8 + 8 * r, 16 + 8 * r)
        lower, upper = slice(7 + 8 * r, 15 + 8 * r), slice(9 + 8 * r, 17 + 8 * r)
        ya, yp, yv, yb, yq, yw = yco[0, here], yco[2, here], yco[4, here], yco[1, lower], yco[3, lower], yco[4, lower]
        for t in range(NTR):
            c, z = cpad[t, here], zpad[t, here]
            s = minmod(roll(c, -1) - c, c - roll(c, 1))
            slope[t, 8 * r : 8 * r + 8] = jnp.where(at_side, at_edge(edge_slope, r, t), s)
            s = minmod(cpad[t, upper] - c, c - cpad[t, lower])
            hpad[t, here] = ya * c + yp * s + yv * z
            gpad[t, here] = yb * c + yq * s + yw * z
        yield True
    for r in range(8):
        here = slice(8 + 8 * r, 16 + 8 * r)
        lower, upper = slice(7 + 8 * r, 15 + 8 * r), slice(9 + 8 * r, 17 + 8 * r)
        part = slice(8 * r, 8 * r + 8)
        xa, xp, xv, xb, xq, xw = [xco[i, part] for i in range(6)]
        wet = mpad[here]
        for t in range(NTR):
            c, z, s = cpad[t, here], zpad[t, here], slope[t, part]
            h = xa * c + xp * s + xv * z
            g = xb * c + xq * s + xw * z
            flux = at_edge(edge_flux, r, t)
            out_east = jnp.where(last_lane, flux, h + roll(g, -1))
            in_west = jnp.where(first_lane, flux, g + roll(h, 1))
            out_north = hpad[t, here] + gpad[t, upper]
            in_south = hpad[t, lower] + gpad[t, here]
            write(t, part, wet * (c - (out_east - in_west) - (out_north - in_south)))
        yield True


def level_scratch():
    padded = pltpu.VMEM((NTR, 80, LANES), F32)
    return [
        padded,
        padded,
        padded,
        pltpu.VMEM((NTR, ROWS, LANES), F32),
        pltpu.VMEM((6, ROWS, LANES), F32),
        pltpu.VMEM((5, 80, LANES), F32),
        pltpu.VMEM((80, LANES), F32),
        pltpu.VMEM((4, 8, LANES), F32),
    ]


def chunk_spans(lo, hi):
    spans, size = [], 4
    while lo < hi:
        end = min(lo + size, hi)
        if hi - end < size:
            end = hi
        spans.append((lo, end))
        lo, size = end, size + 2
    return spans


def deep_kernel(
    first, together, top, tracers, east, north, mask, west_cols, east_cols, own_cols, row_below, row_above, ghost, out,
    cells, flows_e, flows_n, lands, west_v, east_v, own_v, below_v, above_v, ghost_v, results, edges, halo_sem, level_sem, out_sem, *scratch
):
    levels = cells.shape[1]

    def halo_copies():
        pairs = ((row_below, below_v), (row_above, above_v), (west_cols, west_v), (east_cols, east_v), (own_cols, own_v), (ghost, ghost_v))
        return [pltpu.make_async_copy(a, b, halo_sem.at[i]) for i, (a, b) in enumerate(pairs)]

    spans = chunk_spans(first - 1, levels)
    sends = chunk_spans(first, levels)[::-1]
    sends = [(first + levels - hi, first + levels - lo) for lo, hi in sends]

    def cell_copy(i):
        lo, hi = spans[i]
        return pltpu.make_async_copy(tracers.at[:, lo:hi], cells.at[:, lo:hi, 8:72], level_sem.at[0, i])

    def flow_copies(i):
        lo, hi = spans[i]
        pairs = ((east, flows_e), (north, flows_n), (mask, lands))
        return [pltpu.make_async_copy(a.at[lo:hi], b.at[lo:hi], level_sem.at[1 + j, i]) for j, (a, b) in enumerate(pairs)]

    def out_copy(i):
        lo, hi = sends[i]
        return pltpu.make_async_copy(results.at[:, lo - first : hi - first], out.at[:, lo:hi], out_sem.at[i])

    cell_copy(0).start()
    for copy in flow_copies(0) + halo_copies():
        copy.start()
    for i in range(1, len(spans)):
        cell_copy(i).start()
        for copy in flow_copies(i):
            copy.start()
    for copy in halo_copies():
        copy.wait()

    @pl.when(top[0] > 0)
    def _():
        field = lax.broadcasted_iota(jnp.int32, ghost_v.shape, 1)
        above_v[:, 0] = jnp.where(field == 7, 1.0, ghost_v[...])
        above_v[:, 1] = ghost_v[...]

    for lo in range(first, levels, EDGE_LEVELS):
        ks = range(lo, min(lo + EDGE_LEVELS, levels))
        stacked = (8 * len(ks), LANES)
        lane_of_four = lanes_of(stacked) % 4

        def stack(ref, j, h):
            return jnp.concatenate([ref[min(k + j, levels - 1), h] for k in ks], 0)

        slopes, fluxes = edge_values(
            lambda j, h: jnp.where(lane_of_four < 2, stack(west_v, j, h), stack(east_v, j, h)),
            lambda j, h: stack(own_v, j, h),
        )
        for i, k in enumerate(ks):
            edges[k, 0] = slopes[8 * i : 8 * i + 8]
            edges[k, 1] = fluxes[8 * i : 8 * i + 8]
    for copy in flow_copies(0) + [cell_copy(0)]:
        copy.wait()

    def several(i, _):
        k0 = first + i * together
        for i in range(1, len(spans)):

            @pl.when(jnp.logical_and(k0 + together >= spans[i][0], k0 < spans[i][0]))
            def _():
                for copy in flow_copies(i) + [cell_copy(i)]:
                    copy.wait()

        size = len(scratch) // together
        in_step(*[one(k0 + j, scratch[j * size : (j + 1) * size]) for j in range(together)])
        for i in range(len(sends)):

            @pl.when(k0 + together == sends[i][1])
            def _():
                out_copy(i).start()

        return 0

    def one(k, scratch):
        level = {-1: k - 1, 0: k, 1: jnp.minimum(k + 1, levels - 1)}

        def write(t, part, value):
            results[t, k - first, part] = value

        return level_step(
            cells.at[:, k - 1],
            cells.at[:, k],
            cells.at[:, level[1]],
            lambda j, i: below_v[level[j], i],
            lambda j, i: above_v[level[j], i],
            edges[k, 0],
            edges[k, 1],
            flows_e[k],
            flows_n[k],
            lands[k].astype(F32),
            write,
            scratch,
        )

    lax.fori_loop(0, (levels - first) // together, several, 0)
    for i in range(len(sends)):
        out_copy(i).wait()


def deep_levels(first, top, tracers, east, north, mask, west_cols, east_cols, own_cols, row_below, row_above, ghost):
    levels = tracers.shape[1]
    halos = (west_cols, east_cols, own_cols, row_below, row_above, ghost)
    flow = (levels, ROWS, LANES)
    return pl.pallas_call(
        functools.partial(deep_kernel, first, TOGETHER),
        in_specs=[pl.BlockSpec(memory_space=pltpu.SMEM)]
        + [pl.BlockSpec(memory_space=pltpu.HBM)] * 4
        + [pl.BlockSpec(memory_space=pl.ANY)] * 6,
        out_specs=pl.BlockSpec(memory_space=pl.ANY),
        out_shape=jax.ShapeDtypeStruct(tracers.shape, F32),
        scratch_shapes=[
            pltpu.VMEM((NTR, levels, ROWS + 16, LANES), F32),
            pltpu.VMEM(flow, F32),
            pltpu.VMEM(flow, F32),
            pltpu.VMEM(flow, jnp.int32),
        ]
        + [pltpu.VMEM(x.shape, F32) for x in halos]
        + [
            pltpu.VMEM((NTR, levels - first, ROWS, LANES), F32),
            pltpu.VMEM((levels, 2, 8, LANES), F32),
            pltpu.SemaphoreType.DMA((6,)),
            pltpu.SemaphoreType.DMA((4, levels)),
            pltpu.SemaphoreType.DMA((levels,)),
        ]
        + level_scratch() * TOGETHER,
        compiler_params=pltpu.CompilerParams(vmem_limit_bytes=VMEM_LIMIT),
        name="deep_levels",
    )(top, tracers, east, north, mask, *halos)


def expand(x, lane):
    total = x
    for f in range(2, 6):
        total = jnp.where(lane // 4 == f, roll(x, 4 * (f - 1)), total)
    return jnp.where(lane // 4 == 6, roll(x, 16), total)


def pack_rows(tiles, lane):
    packed = []
    for h in range(2):
        total = jnp.zeros((8, LANES), F32)
        for rr in range(4):
            total = jnp.where(lane // 32 == rr, roll(tiles[4 * h + rr], 32 * rr), total)
        packed.append(total)
    return packed


def force_columns(cols, force, lane):
    field = (lane % 32) // 4
    mask = spread(roll(cols, -28), lane % 32)
    tracer_change = mask * (force * jnp.where(field == 0, HEAT_SCALE, FRESH_SCALE * cols))
    return cols + jnp.where(field < 6, tracer_change, jnp.where(field == 6, STRESS_SCALE * force, 0.0))


def force_rows(rows, mask, heat, fresh, tau):
    field = lax.broadcasted_iota(jnp.int32, (8, LANES), 0)
    tracer_change = mask * jnp.where(field == 0, HEAT_SCALE * heat, FRESH_SCALE * fresh * rows)
    return rows + jnp.where(field < 6, tracer_change, jnp.where(field == 6, STRESS_SCALE * tau, 0.0))


def surface_kernel(
    top, arrived, tracers, east, north, mask, west_cols, east_cols, own_cols, row_below, arriving_above, ghost, _, forcing, out,
    row_above, cells, cell_sem, rows_b, rows_a, cols_h, cols_o, *scratch
):
    copy = pltpu.make_async_copy(tracers.at[:, 0:3], cells.at[:, :, 8:72], cell_sem)
    copy.start()
    devices = arrived.shape[0] // (4 * GROUPS)
    stride = 4 * GROUPS
    lane = lanes_of((8, LANES))
    lane_of_four = lane % 4

    def gathered(group, row):
        return arrived[pl.ds(4 * group + row, devices, stride=stride), :]

    labels = gathered(4, 0).T[LABEL_LANE : LABEL_LANE + 16]
    row_id = lax.broadcasted_iota(jnp.int32, (ROWS, devices), 0).astype(F32) + 1.0

    def pick(n):
        return (labels[n : n + 1] == row_id).astype(F32)

    def dot(a, b):
        return jnp.dot(a, b, precision=lax.Precision.HIGHEST, preferred_element_type=F32)

    flux = jnp.zeros((ROWS, 4 * LANES), F32)
    for n in range(4):
        flux += dot(pick(n), jnp.concatenate([gathered(n, f) for f in range(4)], 1))
    fields = [flux[:, LANES * f : LANES * (f + 1)] for f in range(4)]
    for f in range(4):
        forcing[f] = fields[f]
    heat, fresh, tau_x, tau_y = fields

    wide = lanes_of((devices, LANES))
    sides = [gathered(4, f) for f in range(3)]
    beside = jnp.zeros((ROWS, LANES), F32)
    for side in range(2):
        for n in range(4):
            back = -4 * n - 16 * side
            lined = jnp.where(
                wide < 4, roll(sides[0], back), jnp.where(wide < 8, roll(sides[1], back + 4), roll(sides[2], back + 8))
            )
            lined = jnp.where((wide < 12) & (wide % 4 // 2 == side), lined, 0.0)
            beside += dot(pick(4 + 4 * side + n), lined)

    over = [jnp.sum(gathered(5, f), 0, keepdims=True) for f in range(4)]
    under = [jnp.sum(gathered(6, f), 0, keepdims=True) for f in range(4)]
    tau_under = jnp.sum(gathered(4, 3), 0, keepdims=True)
    is_top = top[0] > 0
    field = lax.broadcasted_iota(jnp.int32, (8, LANES), 0)
    for k in range(3):
        row_above[k, 0] = jnp.where(is_top, jnp.where(field == 7, 1.0, ghost[k]), arriving_above[k, 0])
        row_above[k, 1] = jnp.where(is_top, ghost[k], arriving_above[k, 1])

    land = [mask[k].astype(F32) for k in range(2)]
    copy.wait()
    cells[0, 0, 8:72] = cells[0, 0, 8:72] + land[0] * (HEAT_SCALE * heat)
    for t in range(1, NTR):
        c = cells[t, 0, 8:72]
        cells[t, 0, 8:72] = c + land[0] * (FRESH_SCALE * fresh * c)
    rows_b[0] = force_rows(row_below[0, 0], row_below[0, 0, 7:8], under[2], under[3], 0.0)
    rows_b[1] = force_rows(row_below[0, 1], row_below[0, 1, 7:8], under[0], under[1], tau_under)
    near = jnp.where(is_top, row_above[0, 1, 7:8], row_above[0, 0, 7:8])
    rows_a[0] = force_rows(row_above[0, 0], near, over[0], over[1], 0.0)
    rows_a[1] = force_rows(row_above[0, 1], row_above[0, 1, 7:8], over[2], over[3], 0.0)
    own_tiles, halo_tiles = [], []
    for r in range(8):
        part = slice(8 * r, 8 * r + 8)
        mine = jnp.where(lane < 4, roll(heat[part], 2), jnp.where(lane < 8, roll(fresh[part], 6), roll(tau_x[part], 10)))
        own_tiles.append(expand(mine, lane))
        halo_tiles.append(expand(beside[part], lane))
    own_force, halo_force = pack_rows(own_tiles, lane), pack_rows(halo_tiles, lane)
    for h in range(2):
        cols = jnp.where(lane_of_four < 2, west_cols[0, h], east_cols[0, h])
        cols_h[h] = force_columns(cols, halo_force[h], lane)
        cols_o[h] = force_columns(own_cols[0, h], own_force[h], lane)

    def level(k):
        def at(j):
            return max(k + j, 0)

        def write(t, part, value):
            out[t, k, part] = value

        size = len(scratch) // 2
        return level_step(
            cells.at[:, at(-1)],
            cells.at[:, k],
            cells.at[:, k + 1],
            lambda j, i: rows_b[i] if at(j) == 0 else row_below[at(j), i],
            lambda j, i: rows_a[i] if at(j) == 0 else row_above[at(j), i],
            slopes[8 * k : 8 * k + 8],
            fluxes[8 * k : 8 * k + 8],
            east[k] + STRESS_SCALE * tau_x if k == 0 else east[k],
            north[k] + STRESS_SCALE * tau_y if k == 0 else north[k],
            land[k],
            write,
            scratch[size * k : size * (k + 1)],
        )

    def halo_at(k, h):
        return cols_h[h] if k <= 0 else jnp.where(lane_of_four < 2, west_cols[k, h], east_cols[k, h])

    def own_at(k, h):
        return cols_o[h] if k <= 0 else own_cols[k, h]

    slopes, fluxes = edge_values(
        lambda j, h: jnp.concatenate([halo_at(k + j, h) for k in range(2)], 0),
        lambda j, h: jnp.concatenate([own_at(k + j, h) for k in range(2)], 0),
    )
    in_step(level(0), level(1))


def surface_levels(top, arrived, tracers, east, north, mask, west_cols, east_cols, own_cols, row_below, row_above, ghost, done):
    block = lambda n: pl.BlockSpec((NTR, n, ROWS, LANES), lambda i: (0, 0, 0, 0))
    flow = pl.BlockSpec((2, ROWS, LANES), lambda i: (0, 0, 0))
    halo = lambda x: pl.BlockSpec((3,) + x.shape[1:], lambda i: (0,) * x.ndim)
    return pl.pallas_call(
        surface_kernel,
        grid=(1,),
        in_specs=[
            pl.BlockSpec(memory_space=pltpu.SMEM),
            pl.BlockSpec(arrived.shape, lambda i: (0, 0)),
            pl.BlockSpec(memory_space=pltpu.HBM),
            flow,
            flow,
            flow,
        ]
        + [halo(x) for x in (west_cols, east_cols, own_cols, row_below, row_above, ghost)]
        + [pl.BlockSpec(memory_space=pltpu.HBM)],
        out_specs=[pl.BlockSpec((4, ROWS, LANES), lambda i: (0, 0, 0)), block(2)],
        out_shape=[jax.ShapeDtypeStruct((4, ROWS, LANES), F32), jax.ShapeDtypeStruct(tracers.shape, F32)],
        input_output_aliases={12: 1},
        scratch_shapes=[
            pltpu.VMEM((3, 2, 8, LANES), F32),
            pltpu.VMEM((NTR, 3, ROWS + 16, LANES), F32),
            pltpu.SemaphoreType.DMA,
            pltpu.VMEM((2, 8, LANES), F32),
            pltpu.VMEM((2, 8, LANES), F32),
            pltpu.VMEM((2, 8, LANES), F32),
            pltpu.VMEM((2, 8, LANES), F32),
        ]
        + level_scratch() * 2,
        compiler_params=pltpu.CompilerParams(vmem_limit_bytes=VMEM_LIMIT),
        name="surface_levels",
    )(top, arrived, tracers, east, north, mask, west_cols, east_cols, own_cols, row_below, row_above, ghost, done)


def strip_kernel(c, own, west, out):
    low = c[0] % LANES
    levels = own.shape[0]
    lane = lanes_of((levels, 8, LANES))
    joined = jnp.where(lane <= low, own[:, 0], west[:, 0]).reshape(levels * 8, LANES)
    out[...] = reversed_lanes(joined, low).reshape(levels, 8, LANES)


def fold_strip(both, west_cols, c):
    levels = both.shape[0]
    top = pl.BlockSpec((levels, 1, 8, LANES), lambda i: (0, 2, 0, 0))
    return pl.pallas_call(
        strip_kernel,
        grid=(1,),
        in_specs=[pl.BlockSpec(memory_space=pltpu.SMEM), top, top],
        out_specs=pl.BlockSpec((levels, 8, LANES), lambda i: (0, 0, 0)),
        out_shape=jax.ShapeDtypeStruct((levels, 8, LANES), F32),
        name="fold_strip",
    )(c, both, west_cols)


def body(tracers, flow_east, flow_north, sea_mask, atm_fields, remap_weights, remap_src, remap_dst, fold_partner):
    n_lon, n_lat = lax.axis_size("lon"), lax.axis_size("lat")
    devices = n_lon * n_lat
    lon, lat = lax.axis_index("lon"), lax.axis_index("lat")
    c = (fold_partner[0] + lon * LANES) % (n_lon * LANES)
    top = (lat == n_lat - 1).astype(jnp.int32)[None]

    both, own_cols, up, down = pack_halos(tracers, flow_east, flow_north, sea_mask)
    right = [(i, (i + 1) % n_lon) for i in range(n_lon)]
    left = [(j, i) for i, j in right]
    north = [(i, i + 1) for i in range(n_lat - 1)]
    south = [(j, i) for i, j in north]
    west_cols = lax.ppermute(both, "lon", right)
    row_below = lax.ppermute(up, "lat", north)
    row_above = lax.ppermute(down, "lat", south)
    east_cols = lax.ppermute(own_cols, "lon", left)
    atm_fields, _ = lax.optimization_barrier((atm_fields, both))
    outgoing = remap(atm_fields, remap_weights, remap_src, remap_dst, c[None], n_lon, n_lat)
    west_cols, outgoing = lax.optimization_barrier((west_cols, outgoing))
    strip = fold_strip(both, west_cols, c[None])

    def move(b):
        pairs = [(q * n_lat + n_lat - 1, ((b - q) % n_lon) * n_lat + n_lat - 1) for q in range(n_lon)]
        return lambda x: lax.ppermute(x, ("lon", "lat"), pairs)

    ghost = lax.switch(c // LANES, [move(b) for b in range(n_lon)], strip)
    outgoing, ghost, east_cols, row_below, row_above = lax.optimization_barrier(
        (outgoing, ghost, east_cols, row_below, row_above)
    )
    arrived = lax.all_to_all(outgoing, ("lon", "lat"), split_axis=0, concat_axis=0, tiled=True)
    halos = (west_cols, east_cols, own_cols, row_below, row_above, ghost)
    done = deep_levels(2, top, tracers, flow_east, flow_north, sea_mask, *halos)
    arrived = arrived.reshape(devices * 4 * GROUPS, LANES)
    return surface_levels(top, arrived, tracers, flow_east, flow_north, sea_mask, *halos, done)


def solution(mesh):
    placed = (
        P(None, None, "lat", "lon"),
        P(None, "lat", "lon"),
        P(None, "lat", "lon"),
        P(None, "lat", "lon"),
        P(None, ("lon", "lat")),
        P(("lon", "lat"), None, None),
        P(("lon", "lat")),
        P(("lon", "lat")),
        P("lon"),
    )
    return jax.shard_map(
        body,
        mesh=mesh,
        in_specs=placed,
        out_specs=(P(None, "lat", "lon"), P(None, None, "lat", "lon")),
        check_vma=False,
    )
```
